512 devices in a mesh: slab: 128 (over y, z, core), grp: 4 (over x).
Axes of the slice: x: 4, y: 8, z: 8, core: 2. Of those that a mesh axis runs over, the one named last changes fastest.
Arguments:
- u_now: float32 [3, 2048, 32, 128], P(None, 'slab', 'grp'), may hold values from -6 to 6
- u_prev: float32 [3, 2048, 32, 128], P(None, 'slab', 'grp'), may hold values from -6 to 6
- force: float32 [3, 2048, 32, 128], P(None, 'slab', 'grp'), may hold values from -6 to 6
- stiffness: float32 [2048, 32, 128], P('slab', 'grp'), may hold values from 0.5 to 2
- broken: int32 [512, 8, 32], P('slab', 'grp'), may hold values 0 or 1
- flags: int32 [512, 8, 32], P('slab', 'grp'), may hold values 0 or 1
Outputs:
- displacement: float32 [3, 2048, 32, 128], P(None, 'slab', 'grp')
- coeffs: float32 [6, 32, 128, 2048], P(None, 'grp', 'slab')
The draws below stay inside these ranges and needn't reach their ends.
All inputs are finite; a program needn't handle non-finite values. No bound on the sum of `broken` or of `flags` on one device may be relied on, other than what follows from the above.
Results may differ from the reference program's by a relative error of at most 0.0001.
Values sent between devices are 32-bit elements; how exact they have to be, the bound alone decides.
No kernel may reach another device: no remote copies, remote signals or barrier semaphores. Data moves between devices by JAX's collectives and lax.ppermute only.
A program may use at most 64 MiB of HBM per device.

```python
import math
import jax
import jax.numpy as jnp
import numpy as np
from jax import lax

NZ = 128
STEPS = 2
ITERS = 2
LEVELS = 3
NX = 2048
NY = 32


def place_ends(values, stream_key, low, largest):
    longest = values.shape.index(max(values.shape))
    spots = []
    for shift in (0, 1):
        where = [jax.random.randint(jax.random.fold_in(stream_key, axis), (), 0, length) for axis, length in enumerate(values.shape)]
        where[longest] = (where[longest] + shift) % values.shape[longest]
        spots.append(tuple(where))
    return values.at[spots[0]].set(low).at[spots[1]].set(largest)


def level_of(stream_key, extent, split, least, largest):
    gain, own = 1.0, jax.random.fold_in(stream_key, 6)
    for axis_at, parts in split:
        steps = jnp.exp(jax.random.uniform(jax.random.fold_in(own, axis_at), (parts,), jnp.float32, least / len(split), largest / len(split)))
        gain = gain * jnp.repeat(steps, extent[axis_at] // parts).reshape([-1 if axis == axis_at else 1 for axis in range(len(extent))])
    return gain


def gaussian(rng, dims, deviation, reach, split=(), held_as=jnp.bfloat16):
    loudness = level_of(rng, dims, split, -0.22, 0.18) if split else 1.0
    entries = jax.random.normal(rng, dims, jnp.float32) * deviation * loudness
    return jnp.minimum(jnp.maximum(entries, -reach), reach).astype(held_as)


def setup_inputs(seed: int = 0) -> dict:
    key_of = jax.random.split(jax.random.key(seed), 7)
    u_now = gaussian(key_of[0], (3, NX, NY, NZ), 1.0, 6.0, ((1, 128), (2, 4)), jnp.float32)
    u_prev = gaussian(key_of[1], (3, NX, NY, NZ), 1.0, 6.0, ((1, 128), (2, 4)), jnp.float32)
    force = gaussian(key_of[2], (3, NX, NY, NZ), 1.0, 6.0, ((1, 128), (2, 4)), jnp.float32)
    stiffness = jnp.clip(jnp.exp(math.log(2.0) - 1.3862944 * jax.random.uniform(key_of[3], (NX, NY, NZ), jnp.float32) ** level_of(key_of[3], (NX, NY, NZ), ((0, 128), (1, 4)), -0.2, 0.2)), 0.5, 2.0)
    broken = place_ends((jax.random.randint(key_of[4], (NX // 4, NY // 4, NZ // 4), 0, 4) < 1).astype(jnp.int32), jax.random.fold_in(key_of[4], 1), 0, 1)
    flags = place_ends((jax.random.randint(key_of[5], (NX // 4, NY // 4, NZ // 4), 0, 3) < 2).astype(jnp.int32), jax.random.fold_in(key_of[5], 1), 0, 1)
    return {"u_now": u_now, "u_prev": u_prev, "force": force, "stiffness": stiffness, "broken": broken, "flags": flags}


SPRING_NORMAL = 1.0
SPRING_SHEAR = 0.4
MASS_TERM = 1.0
CRACK_CUT = 0.9

def cosine_table():
    freq = np.arange(4)[:, None]
    place = np.arange(4)[None, :]
    factor = np.where(freq == 0, 0.5, np.sqrt(0.5))
    return factor * np.cos(np.pi * (2 * place + 1) * freq / 8.0)

def spread(mask):
    values = mask.astype(jnp.float32)
    size_a, size_b, size_c = values.shape
    wide = jnp.broadcast_to(values[:, None, :, None, :, None], (size_a, 4, size_b, 4, size_c, 4))
    return wide.reshape(size_a * 4, size_b * 4, size_c * 4)

def sides(padded, axis_index):
    leading = padded.ndim - 3

    def cut(offset):
        index_list = [slice(None)] * leading + [slice(1, -1)] * 3
        length = padded.shape[leading + axis_index]
        index_list[leading + axis_index] = slice(1 + offset, length - 1 + offset)
        return padded[tuple(index_list)]
    return (cut(1), cut(-1))

def springs(field, weight, field_pad, weight_pad):
    result = MASS_TERM * field
    for axis_index in range(3):
        upper_v, lower_v = sides(field_pad, axis_index)
        upper_w, lower_w = sides(weight_pad, axis_index)
        k_upper = 0.5 * (weight + upper_w)
        k_lower = 0.5 * (weight + lower_w)
        change = k_upper * (field - upper_v) + k_lower * (field - lower_v)
        coupling = jnp.array([SPRING_NORMAL if comp == axis_index else SPRING_SHEAR for comp in range(3)], jnp.float32).reshape(3, 1, 1, 1)
        result = result + coupling * change
    return result

def stresses(field, carry, field_pad):
    rows_out = []
    for axis_index in range(3):
        upper_v, lower_v = sides(field_pad, axis_index)
        rows_out.append(SPRING_NORMAL * carry * 0.5 * (upper_v[axis_index] - lower_v[axis_index]))
    return jnp.stack(rows_out)

def lift(signal):
    even = signal[..., 0::2]
    odd = signal[..., 1::2]
    detail = odd - 0.5 * (even + jnp.roll(even, -1, axis=-1))
    approx = even + 0.25 * (jnp.roll(detail, 1, axis=-1) + detail)
    return (approx, detail)

def wavelet(signal):
    pieces = []
    approx = signal
    for level_index in range(LEVELS):
        approx, detail = lift(approx)
        pieces.insert(0, detail)
    return jnp.concatenate([approx] + pieces, axis=-1)

def block_transform(fields):
    table = jnp.asarray(cosine_table(), jnp.float32)
    chans, size_x, size_y, size_z = fields.shape
    grid = fields.reshape(chans, size_x // 4, 4, size_y // 4, 4, size_z // 4, 4)
    grid = jnp.einsum('ai,hpiqjrk->hpaqjrk', table, grid, precision=lax.Precision.HIGHEST)
    grid = jnp.einsum('bj,hpaqjrk->hpaqbrk', table, grid, precision=lax.Precision.HIGHEST)
    grid = jnp.einsum('ck,hpaqbrk->hpaqbrc', table, grid, precision=lax.Precision.HIGHEST)
    return grid.reshape(fields.shape)

def reference(u_now, u_prev, force, stiffness, broken, flags):
    weight = stiffness * (1.0 - CRACK_CUT * spread(broken))
    carry = spread(flags) * weight
    weight_pad = jnp.pad(weight, 1)

    def operate(field):
        field_pad = jnp.pad(field, ((0, 0), (1, 1), (1, 1), (1, 1)))
        return springs(field, weight, field_pad, weight_pad)
    for step_index in range(STEPS):
        rhs = MASS_TERM * (2.0 * u_now - u_prev) + force
        guess = u_now
        residual = rhs - operate(guess)
        direction = residual
        norm_now = jnp.sum(residual * residual)
        for turn_index in range(ITERS):
            image = operate(direction)
            alpha = norm_now / jnp.sum(direction * image)
            guess = guess + alpha * direction
            residual = residual - alpha * image
            if turn_index + 1 < ITERS:
                norm_next = jnp.sum(residual * residual)
                direction = residual + norm_next / norm_now * direction
                norm_now = norm_next
        u_prev = u_now
        u_now = guess
    field_pad = jnp.pad(u_now, ((0, 0), (1, 1), (1, 1), (1, 1)))
    fields = jnp.concatenate([u_now, stresses(u_now, carry, field_pad)], axis=0)
    blockc = block_transform(fields)
    coeffs = wavelet(jnp.transpose(blockc, (0, 2, 3, 1)))
    return (u_now, coeffs)
```

```python
import jax
import jax.numpy as jnp
import numpy as np
from jax import lax
from jax.experimental import pallas as pl
from jax.experimental.pallas import tpu as pltpu
from jax.sharding import PartitionSpec as P

SPRING_SHEAR = 0.4
CRACK_CUT = 0.9
SHIFT = 2.5
F32 = jnp.float32
NB = 16
HIGHEST = lax.Precision.HIGHEST


def cosine_table():
    freq = np.arange(4)[:, None]
    place = np.arange(4)[None, :]
    factor = np.where(freq == 0, 0.5, np.sqrt(0.5))
    return factor * np.cos(np.pi * (2 * place + 1) * freq / 8.0)


def lift_np(signal):
    even, odd = signal[..., 0::2], signal[..., 1::2]
    detail = odd - 0.5 * (even + np.roll(even, -1, axis=-1))
    approx = even + 0.25 * (np.roll(detail, 1, axis=-1) + detail)
    return approx, detail


def wavelet_tables():
    size = 2048
    eye = np.eye(size)
    a1, d1 = lift_np(eye)
    a2, d2 = lift_np(a1)
    a3, d3 = lift_np(a2)
    lane = np.arange(128)
    place = (lane % 8) * 16 + lane // 8

    def rows(first, count):
        return np.concatenate([((first + t) % 16) * 128 + place for t in range(count)])

    w1 = d1[rows(0, 3)][:, :128]
    w2 = d2[rows(3, 6)][:, 128:256]
    w3 = np.concatenate([a3[rows(7, 10)][:, 128:], d3[rows(7, 10)][:, 128:]], axis=1)
    return [np.asarray(w, np.float32) for w in (w1, w2, w3)]


def sub_iota():
    return lax.broadcasted_iota(jnp.int32, (8, 128), 0)


def rot(tile, shift, axis):
    return pltpu.roll(tile, shift % tile.shape[axis], axis)


def pack_kernel(u, up, f, st, br, fl, m_up, m_dn, rhs, dif, wt, car):
    sub = sub_iota()
    low = sub < 4
    spread = (
        lax.broadcasted_iota(jnp.int32, (32, 128), 1) // 4
        == lax.broadcasted_iota(jnp.int32, (32, 128), 0)
    ).astype(F32)
    for p in range(4):
        wide_b = jnp.dot(br[p].astype(F32), spread, preferred_element_type=F32)
        wide_f = jnp.dot(fl[p].astype(F32), spread, preferred_element_type=F32)
        cut = 1.0 - CRACK_CUT * jnp.where(low, wide_b[0:1, :], wide_b[1:2, :])
        on = jnp.where(low, wide_f[0:1, :], wide_f[1:2, :])
        for x in range(4 * p, 4 * p + 4):
            w = st[x] * cut
            wt[x] = w
            car[x] = 0.5 * on * w
            uu, rr, dd = [], [], []
            for c in range(3):
                a = u[c, x]
                b = up[c, x]
                uu.append(a)
                rr.append((2.0 * a - b) + f[c, x])
                dd.append(a - b)
                rhs[c, x] = rr[c]
                dif[c, x] = dd[c]
            u1, w4, r1 = rot(uu[1], 4, 0), rot(w, 4, 0), rot(rr[1], 4, 0)
            m_up[x, 0] = jnp.where(low, u1, uu[0])
            m_up[x, 1] = jnp.where(low, w4, uu[2])
            m_up[x, 2] = jnp.where(low, r1, rr[0])
            extra = jnp.where(sub == 0, rot(uu[0], -3, 0), jnp.where(sub == 1, rot(uu[1], -2, 0), jnp.where(sub == 2, rot(uu[2], -1, 0), w)))
            m_up[x, 3] = jnp.where(low, extra, rr[2])
            m_up[x, 4] = jnp.where(sub >= 6, dd[0], jnp.where(sub >= 4, rot(dd[1], -2, 0), rot(dd[2], 4, 0)))
            m_dn[x, 0] = jnp.where(low, uu[0], u1)
            m_dn[x, 1] = jnp.where(low, uu[2], w4)
            m_dn[x, 2] = jnp.where(low, rr[0], r1)
            extra = jnp.where(sub == 4, uu[0], jnp.where(sub == 5, rot(uu[1], 1, 0), jnp.where(sub == 6, rot(uu[2], 2, 0), rot(w, 3, 0))))
            m_dn[x, 3] = jnp.where(low, rr[2], extra)
            m_dn[x, 4] = jnp.where(sub < 2, dd[0], jnp.where(sub < 4, rot(dd[1], 2, 0), rot(dd[2], 4, 0)))


def unpack(hi, lo, x, low):
    h0, h1, h2, h3, h4 = (hi[x, t] for t in range(5))
    l0, l1, l2, l3, l4 = (lo[x, t] for t in range(5))
    u0 = jnp.where(low, h0, l0)
    u1 = rot(jnp.where(low, l0, h0), 4, 0)
    u2 = jnp.where(low, h1, l1)
    w = rot(jnp.where(low, l1, h1), 4, 0)
    r0 = jnp.where(low, h2, l2)
    r1 = rot(jnp.where(low, l2, h2), 4, 0)
    r2 = jnp.where(low, h3, l3)
    d0 = jnp.where(low, h4, l4)
    d1 = jnp.where(low, rot(h4, -2, 0), rot(l4, 2, 0))
    d2 = rot(jnp.where(low, l4, h4), 4, 0)
    return (u0, u1, u2), (r0, r1, r2), (d0, d1, d2), w


def face_slots():
    slots, at = {}, 0
    for name, comps, own, halo in (("u", 3, 5, 4), ("r", 3, 4, 3), ("d", 3, 2, 1), ("w", 1, 5, 4)):
        for c in range(comps):
            for k in range(own):
                slots[name, c, k, 0] = at
                at += 1
            for k in range(halo):
                slots[name, c, k, 1] = at
                at += 1
    return slots, at


SLOTS, N_SLOTS = face_slots()


def face_kernel(u, rhs, dif, wt, hi, lo, q_up, q_dn):
    low = sub_iota() < 4
    for out, row in ((q_up, lambda k: NB - 1 - k), (q_dn, lambda k: k)):
        for k in range(5):
            x = row(k)
            hu, hr, hd, hw = unpack(hi, lo, x, low)
            for name, own, halo in (("u", u, hu), ("r", rhs, hr), ("d", dif, hd)):
                for c in range(3):
                    if (name, c, k, 0) in SLOTS:
                        out[SLOTS[name, c, k, 0]] = own[c, x]
                    if (name, c, k, 1) in SLOTS:
                        out[SLOTS[name, c, k, 1]] = halo[c]
            out[SLOTS["w", 0, k, 0]] = wt[x]
            if ("w", 0, k, 1) in SLOTS:
                out[SLOTS["w", 0, k, 1]] = hw


def roll_y_up(pair, sub):
    a, b = rot(pair[0], -1, 0), rot(pair[1], -1, 0)
    return jnp.where(sub == 7, b, a), jnp.where(sub == 7, a, b)


def roll_y_dn(pair, sub):
    a, b = rot(pair[0], 1, 0), rot(pair[1], 1, 0)
    return jnp.where(sub == 0, b, a), jnp.where(sub == 0, a, b)


def pair_of(ref, *lead):
    return ref[(*lead, slice(0, 8))], ref[(*lead, slice(8, 16))]


def put(ref, pair, *lead):
    ref[(*lead, slice(0, 8))] = pair[0]
    ref[(*lead, slice(8, 16))] = pair[1]


def krylov_kernel(u, rhs, dif, wt, hi, lo, q_lo, q_hi, ub, r0, r1, r2, r3, v0, v1, mom, ue, we, re, de, kk):
    sub = sub_iota()
    lane = lax.broadcasted_iota(jnp.int32, (8, 128), 1)
    low = sub < 4
    zero = jnp.zeros((8, 128), F32)

    for k in range(5):
        for q, side in ((q_lo, lambda h, k: h - 1 - k), (q_hi, lambda h, k: h + NB + k)):
            for c in range(3):
                for name, ref, h in (("u", ue, 5), ("r", re, 4), ("d", de, 2)):
                    if (name, c, k, 0) in SLOTS:
                        halo = SLOTS.get((name, c, k, 1))
                        put(ref, (q[SLOTS[name, c, k, 0]], zero if halo is None else q[halo]), c, side(h, k))
            halo = SLOTS.get(("w", 0, k, 1))
            put(we, (q[SLOTS["w", 0, k, 0]], zero if halo is None else q[halo]), side(5, k))

    def fill(x, carry):
        hu, hr, hd, hw = unpack(hi, lo, x, low)
        for c in range(3):
            put(ue, (u[c, x], hu[c]), c, x + 5)
            put(re, (rhs[c, x], hr[c]), c, x + 4)
            put(de, (dif[c, x], hd[c]), c, x + 2)
        put(we, (wt[x], hw), x + 5)
        return carry

    lax.fori_loop(0, NB, fill, 0, unroll=2)

    def edges(x, ends):
        w = pair_of(we, x + 5)
        wxp, wxm = pair_of(we, x + 6), pair_of(we, x + 4)
        wyp, wym = roll_y_up(w, sub), roll_y_dn(w, sub)
        if ends is not None:
            wyp = (wyp[0], jnp.where(sub == 3, ends[0], wyp[1]))
            wym = (wym[0], jnp.where(sub == 4, ends[1], wym[1]))
        for t in range(2):
            rows = slice(8 * t, 8 * t + 8)
            inside = jnp.where(w[t] > 0.0, 0.5 * SPRING_SHEAR, 0.0)
            wzp = jnp.where(lane == 127, 0.0, rot(w[t], -1, 1))
            wzm = jnp.where(lane == 0, 0.0, rot(w[t], 1, 1))
            xp, xm, yp, ym, zp, zm = ((w[t] + o) * inside for o in (wxp[t], wxm[t], wyp[t], wym[t], wzp, wzm))
            sums = (xp + xm, yp + ym, zp + zm)
            base = (1.0 - SHIFT) + (sums[0] + sums[1] + sums[2])
            for i, val in enumerate((xp, xm, yp, ym, jnp.where(lane == 127, 0.0, zp), jnp.where(lane == 0, 0.0, zm))):
                kk[i, x + 4, rows] = val
            for c in range(3):
                kk[6 + c, x + 4, rows] = base + 1.5 * sums[c]

    def own_edges(x, carry):
        edges(x, (hi[x, 3][7:8, :], lo[x, 3][3:4, :]))
        return carry

    def far_edges(i, carry):
        edges(i - 4, None)
        edges(i + NB, None)
        return carry

    lax.fori_loop(0, 4, far_edges, 0)
    lax.fori_loop(0, NB, own_edges, 0, unroll=2)

    def apply_b(ref, h, x, tiles=(0, 1), ends=None):
        k = [[kk[i, x + 4, 8 * t : 8 * t + 8] if t in tiles else None for t in range(2)] for i in range(9)]
        out, mids = [], []
        for c in range(3):
            mid = pair_of(ref, c, x + h)
            yp, ym = roll_y_up(mid, sub), roll_y_dn(mid, sub)
            if ends is not None:
                yp = (yp[0], jnp.where(sub == 3, ends[0][c], yp[1]))
                ym = (ym[0], jnp.where(sub == 4, ends[1][c], ym[1]))
            res = [None, None]
            for t in tiles:
                rows = slice(8 * t, 8 * t + 8)
                sx = k[0][t] * ref[c, x + h + 1, rows] + k[1][t] * ref[c, x + h - 1, rows]
                sy = k[2][t] * yp[t] + k[3][t] * ym[t]
                sz = k[4][t] * rot(mid[t], -1, 1) + k[5][t] * rot(mid[t], 1, 1)
                res[t] = k[6 + c][t] * mid[t] - ((sx + sy) + (sz + 1.5 * (sx, sy, sz)[c]))
            out.append(res)
            mids.append(mid)
        return out, mids

    def first(x, ends, with_v):
        bu, mids = apply_b(ue, 5, x, ends=ends)
        for c in range(3):
            rh = pair_of(re, c, x + 4)
            res = [rh[t] - (bu[c][t] + SHIFT * mids[c][t]) for t in range(2)]
            put(r0, res, c, x + 4)
            if with_v:
                d = pair_of(de, c, x + 2)
                put(v0, [res[t] - d[t] for t in range(2)], c, x + 2)

    def first_own(x, carry):
        h3, l3 = hi[x, 3], lo[x, 3]
        first(x, ([h3[4 + c : 5 + c, :] for c in range(3)], [l3[c : c + 1, :] for c in range(3)]), True)
        for c in range(3):
            put(ub, pair_of(ue, c, x + 5), c, x + 1)
        return carry

    for x in (-4, -3, NB + 2, NB + 3):
        first(x, None, False)
    for x in (-2, -1, NB, NB + 1):
        first(x, None, True)
    for c in range(3):
        put(ub, pair_of(ue, c, 4), c, 0)
        put(ub, pair_of(ue, c, NB + 5), c, NB + 1)
    lax.fori_loop(0, NB, first_own, 0)

    def power(src, h, dst):
        def row(x, carry):
            out, _ = apply_b(src, h, x)
            for c in range(3):
                put(dst, out[c], c, x + h - 1)
            return carry

        lax.fori_loop(1 - h, NB + h - 1, row, 0, unroll=2)

    power(r0, 4, r1)
    power(v0, 2, v1)
    power(r1, 3, r2)
    power(r2, 2, r3)

    def dots(x, acc):
        r4, _ = apply_b(r3, 1, x, tiles=(0,))
        v2, _ = apply_b(v1, 1, x, tiles=(0,))
        acc = list(acc)
        for c in range(3):
            a = [ref[c, x + h, 0:8] for ref, h in ((r0, 4), (r1, 3), (r2, 2), (r3, 1))] + [r4[c][0]]
            b = [v0[c, x + 2, 0:8], v1[c, x + 1, 0:8], v2[c][0]]
            terms = [a[k // 2] * a[(k + 1) // 2] for k in range(8)]
            terms += [b[(k + 1) // 2] * a[k // 2] for k in range(5)] + [b[2] * a[3]]
            terms += [b[k // 2] * b[(k + 1) // 2] for k in range(4)]
            acc = [s + t for s, t in zip(acc, terms)] if c or True else acc
        return tuple(acc)

    acc = lax.fori_loop(0, NB, dots, (zero,) * 18)
    lane_row = lax.broadcasted_iota(jnp.int32, (1, 128), 1)
    line = jnp.zeros((1, 128), F32)
    for k in range(18):
        line = jnp.where(lane_row == k, jnp.sum(jnp.sum(acc[k], axis=0, keepdims=True), axis=1, keepdims=True), line)
    mom[...] = jnp.broadcast_to(line, mom.shape)


def two_iterations(m):
    alpha = m[0] / (SHIFT * m[0] + m[1])
    p0, p1 = 1.0 - SHIFT * alpha, -alpha
    new = p0 * p0 * m[0] + 2.0 * p0 * p1 * m[1] + p1 * p1 * m[2]
    e0, e1 = p0 + new / m[0], p1
    d0 = e0 * e0 * m[0] + 2.0 * e0 * e1 * m[1] + e1 * e1 * m[2]
    d1 = e0 * e0 * m[1] + 2.0 * e0 * e1 * m[2] + e1 * e1 * m[3]
    again = new / (SHIFT * d0 + d1)
    return alpha + again * e0, again * e1


def code_kernel(ub, r0, r1, r2, r3, v0, v1, mom, car, mix, tz, disp, code, uf, fl):
    sub = sub_iota()
    lane = lax.broadcasted_iota(jnp.int32, (8, 128), 1)
    total = jnp.sum(mom[...], axis=0, keepdims=True)
    lane_row = lax.broadcasted_iota(jnp.int32, (1, 128), 1)
    m = [jnp.sum(jnp.where(lane_row == k, total, 0.0), axis=1, keepdims=True) for k in range(18)]
    rr, vr, vv = m[:8], m[8:14], m[14:]
    a0, a1 = two_iterations(rr)
    g = (a0 * (2.0 - SHIFT), a1 * (2.0 - SHIFT) - a0, -a1)
    mix2 = []
    for k in range(4):
        s = vv[k]
        for i in range(3):
            s = s + 2.0 * g[i] * vr[k + i]
            for j in range(3):
                s = s + g[i] * g[j] * rr[k + i + j]
        mix2.append(s)
    b0, b1 = two_iterations(mix2)
    coef = [b0, b1, a0 + b0 * g[0], a1 + b0 * g[1] + b1 * g[0], b0 * g[2] + b1 * g[1], b1 * g[2]]
    coef = [jnp.broadcast_to(v, (8, 128)) for v in coef]
    parts = ((v0, 2), (v1, 1), (r0, 4), (r1, 3), (r2, 2), (r3, 1))

    def combine(i, carry):
        for c in range(3):
            for t in range(2):
                rows = slice(8 * t, 8 * t + 8)
                s = ub[c, i, rows]
                for w, (ref, h) in zip(coef, parts):
                    s = s + w * ref[c, i + h - 1, rows]
                uf[c, i, rows] = s
        return carry

    lax.fori_loop(0, NB + 2, combine, 0, unroll=2)

    def stress(x, carry):
        k = car[x]
        for c in range(3):
            own = uf[c, x + 1, 0:8]
            disp[c, x] = own
            fl[c, x] = own
        fl[3, x] = k * (uf[0, x + 2, 0:8] - uf[0, x, 0:8])
        y = pair_of(uf, 1, x + 1)
        fl[4, x] = k * (roll_y_up(y, sub)[0] - roll_y_dn(y, sub)[0])
        z = uf[2, x + 1, 0:8]
        fl[5, x] = k * (jnp.where(lane == 127, 0.0, rot(z, -1, 1)) - jnp.where(lane == 0, 0.0, rot(z, 1, 1)))
        return carry

    lax.fori_loop(0, NB, stress, 0, unroll=2)
    for ch in range(6):
        field = fl[ch].reshape(128, 128)
        xy = jnp.dot(mix[...], field, precision=HIGHEST, preferred_element_type=F32)
        out = lax.dot_general(tz[...], xy, (((1,), (1,)), ((), ())), precision=HIGHEST, preferred_element_type=F32)
        for i in range(16):
            code[pl.ds(48 * i + ch, 8, stride=6), :] = out[8 * i : 8 * i + 8]


def wavelet_kernel(got, w1, w2, w3, out, xs):
    sub = sub_iota()
    lane = lax.broadcasted_iota(jnp.int32, (8, 128), 1)
    for j in range(16):
        for ch in range(6):
            tile = got[pl.ds(48 * j + ch, 8, stride=6), :]
            for b in range(3):
                step = 1 << b
                s_bit, l_bit = (sub // step) % 2, (lane // step) % 2
                up = rot(rot(tile, -step, 0), step, 1)
                down = rot(rot(tile, step, 0), -step, 1)
                tile = jnp.where(s_bit == l_bit, tile, jnp.where(s_bit == 0, up, down))
            xs[8 * ch : 8 * ch + 8, 128 * j : 128 * j + 128] = tile

    def window(first, count):
        return jnp.concatenate([xs[:, 128 * ((first + t) % 16) : 128 * ((first + t) % 16) + 128] for t in range(count)], axis=1)

    def emit(value, tile):
        for ch in range(6):
            out[pl.ds(128 * ch + tile, 8, stride=16), :] = value[8 * ch : 8 * ch + 8]

    for q in range(8):
        emit(jnp.dot(window(2 * q, 3), w1[...], precision=HIGHEST, preferred_element_type=F32), 8 + q)
    for q in range(4):
        emit(jnp.dot(window(4 * q + 15, 6), w2[...], precision=HIGHEST, preferred_element_type=F32), 4 + q)
    for q in range(2):
        both = jnp.dot(window(8 * q + 15, 10), w3[...], precision=HIGHEST, preferred_element_type=F32)
        emit(both[:, :128], q)
        emit(both[:, 128:], 2 + q)


def call(kernel, outs, scratch=()):
    return pl.pallas_call(
        kernel,
        out_shape=[jax.ShapeDtypeStruct(s, F32) for s in outs],
        scratch_shapes=[pltpu.VMEM(s, F32) for s in scratch],
        compiler_params=pltpu.CompilerParams(vmem_limit_bytes=40 * 2**20),
    )


def body(u_now, u_prev, force, stiffness, broken, flags):
    n_slab, n_grp = lax.axis_size("slab"), lax.axis_size("grp")
    total = n_slab * n_grp
    block, one = (3, NB, 8, 128), (NB, 8, 128)
    m_up, m_dn, rhs, dif, wt, car = call(
        pack_kernel, [(NB, 5, 8, 128)] * 2 + [block, block, one, one]
    )(u_now, u_prev, force, stiffness, broken, flags)
    up = lambda n: [(i, i + 1) for i in range(n - 1)]
    down = lambda n: [(i + 1, i) for i in range(n - 1)]
    lo = lax.ppermute(m_up, "grp", up(n_grp))
    hi = lax.ppermute(m_dn, "grp", down(n_grp))
    q_up, q_dn = call(face_kernel, [(N_SLOTS, 8, 128)] * 2)(u_now, rhs, dif, wt, hi, lo)
    q_lo = lax.ppermute(q_up, "slab", up(n_slab))
    q_hi = lax.ppermute(q_dn, "slab", down(n_slab))
    wide = lambda h: (3, NB + 2 * h, 16, 128)
    *basis, mom = call(
        krylov_kernel,
        [wide(1), wide(4), wide(3), wide(2), wide(1), wide(2), wide(1), (total, 128)],
        [wide(5), wide(5)[1:], wide(4), wide(2), (9, NB + 8, 16, 128)],
    )(u_now, rhs, dif, wt, hi, lo, q_lo, q_hi)
    mom = lax.all_to_all(mom.reshape(total, 1, 128), ("slab", "grp"), 0, 0, tiled=True).reshape(total, 128)
    table = cosine_table()
    mix = jnp.asarray(np.kron(np.kron(np.eye(4), table), np.kron(np.eye(2), table)), F32)
    tz = jnp.asarray(np.kron(np.eye(32), table), F32)
    disp, code = call(
        code_kernel, [block, (768, 128)], [wide(1), (6, NB, 8, 128)]
    )(*basis, mom, car, mix, tz)
    got = lax.all_to_all(code.reshape(n_slab, 1, 768), "slab", 0, 0, tiled=True).reshape(768, 128)
    (coeffs,) = call(wavelet_kernel, [(768, 128)], [(48, 2048)])(got, *(jnp.asarray(w) for w in wavelet_tables()))
    return (disp, coeffs.reshape(6, 8, 1, 2048))


def solution(mesh):
    return jax.shard_map(
        body,
        mesh=mesh,
        in_specs=(
            P(None, "slab", "grp", None),
            P(None, "slab", "grp", None),
            P(None, "slab", "grp", None),
            P("slab", "grp", None),
            P("slab", "grp", None),
            P("slab", "grp", None),
        ),
        out_specs=(P(None, "slab", "grp", None), P(None, "grp", "slab", None)),
        check_vma=False,
    )
```

```python
import jax
import jax.numpy as jnp
import numpy as np
from jax import lax
from jax.experimental import pallas as pl
from jax.experimental.pallas import tpu as pltpu
from jax.sharding import PartitionSpec as P

SPRING_SHEAR = 0.4
CRACK_CUT = 0.9
SHIFT = 2.5
F32 = jnp.float32
BF16 = jnp.bfloat16
NB = 16


def cosine_table():
    freq = np.arange(4)[:, None]
    place = np.arange(4)[None, :]
    factor = np.where(freq == 0, 0.5, np.sqrt(0.5))
    return factor * np.cos(np.pi * (2 * place + 1) * freq / 8.0)


def lift_np(signal):
    even, odd = signal[..., 0::2], signal[..., 1::2]
    detail = odd - 0.5 * (even + np.roll(even, -1, axis=-1))
    approx = even + 0.25 * (np.roll(detail, 1, axis=-1) + detail)
    return approx, detail


def wavelet_tables():
    size = 2048
    eye = np.eye(size)
    a1, d1 = lift_np(eye)
    a2, d2 = lift_np(a1)
    a3, d3 = lift_np(a2)
    lane = np.arange(128)
    place = (lane % 8) * 16 + lane // 8

    def rows(first, count):
        return np.concatenate([((first + t) % 16) * 128 + place for t in range(count)])

    w1 = d1[rows(0, 3)][:, :128]
    w2 = d2[rows(3, 6)][:, 128:256]
    w3 = np.concatenate([a3[rows(7, 10)][:, 128:], d3[rows(7, 10)][:, 128:]], axis=1)
    return [np.asarray(w, np.float32) for w in (w1, w2, w3)]


def two_parts(table):
    high = np.asarray(table, BF16)
    return jnp.stack([jnp.asarray(high), jnp.asarray(np.asarray(table - high.astype(np.float64), BF16))])


def sub_iota():
    return lax.broadcasted_iota(jnp.int32, (8, 128), 0)


def split(value):
    high = value.astype(BF16)
    return high, (value - high.astype(F32)).astype(BF16)


def rot(tile, shift, axis):
    return pltpu.roll(tile, shift % tile.shape[axis], axis)


def pack_kernel(u_in, up_in, f_in, st_in, br_in, fl_in, m_up, m_dn, rhs, dif, wt, car, u, up, f, st, br, fl, sems):
    pairs = ((br_in, br), (fl_in, fl), (st_in, st), (u_in, u), (up_in, up), (f_in, f))
    copies = [pltpu.make_async_copy(a, b, sems.at[i]) for i, (a, b) in enumerate(pairs)]
    for copy in copies:
        copy.start()
    for copy in copies:
        copy.wait()
    sub = sub_iota()
    low = sub < 4
    spread = (
        lax.broadcasted_iota(jnp.int32, (32, 128), 1) // 4
        == lax.broadcasted_iota(jnp.int32, (32, 128), 0)
    ).astype(F32)
    for p in range(4):
        wide_b = jnp.dot(br[p].astype(F32), spread, preferred_element_type=F32)
        wide_f = jnp.dot(fl[p].astype(F32), spread, preferred_element_type=F32)
        cut = 1.0 - CRACK_CUT * jnp.where(low, wide_b[0:1, :], wide_b[1:2, :])
        on = jnp.where(low, wide_f[0:1, :], wide_f[1:2, :])
        for x in range(4 * p, 4 * p + 4):
            w = st[x] * cut
            wt[x] = w
            car[x] = 0.5 * on * w
            uu, rr, dd = [], [], []
            for c in range(3):
                a = u[c, x]
                b = up[c, x]
                uu.append(a)
                rr.append((2.0 * a - b) + f[c, x])
                dd.append(a - b)
                rhs[c, x] = rr[c]
                dif[c, x] = dd[c]
            u1, w4, r1 = rot(uu[1], 4, 0), rot(w, 4, 0), rot(rr[1], 4, 0)
            m_up[x, 0] = jnp.where(low, u1, uu[0])
            m_up[x, 1] = jnp.where(low, w4, uu[2])
            m_up[x, 2] = jnp.where(low, r1, rr[0])
            extra = jnp.where(sub == 0, rot(uu[0], -3, 0), jnp.where(sub == 1, rot(uu[1], -2, 0), jnp.where(sub == 2, rot(uu[2], -1, 0), w)))
            m_up[x, 3] = jnp.where(low, extra, rr[2])
            m_up[x, 4] = jnp.where(sub >= 6, dd[0], jnp.where(sub >= 4, rot(dd[1], -2, 0), rot(dd[2], 4, 0)))
            m_dn[x, 0] = jnp.where(low, uu[0], u1)
            m_dn[x, 1] = jnp.where(low, uu[2], w4)
            m_dn[x, 2] = jnp.where(low, rr[0], r1)
            extra = jnp.where(sub == 4, uu[0], jnp.where(sub == 5, rot(uu[1], 1, 0), jnp.where(sub == 6, rot(uu[2], 2, 0), rot(w, 3, 0))))
            m_dn[x, 3] = jnp.where(low, rr[2], extra)
            m_dn[x, 4] = jnp.where(sub < 2, dd[0], jnp.where(sub < 4, rot(dd[1], 2, 0), rot(dd[2], 4, 0)))


def unpack(hi, lo, x, low):
    h0, h1, h2, h3, h4 = (hi[x, t] for t in range(5))
    l0, l1, l2, l3, l4 = (lo[x, t] for t in range(5))
    u0 = jnp.where(low, h0, l0)
    u1 = rot(jnp.where(low, l0, h0), 4, 0)
    u2 = jnp.where(low, h1, l1)
    w = rot(jnp.where(low, l1, h1), 4, 0)
    r0 = jnp.where(low, h2, l2)
    r1 = rot(jnp.where(low, l2, h2), 4, 0)
    r2 = jnp.where(low, h3, l3)
    d0 = jnp.where(low, h4, l4)
    d1 = jnp.where(low, rot(h4, -2, 0), rot(l4, 2, 0))
    d2 = rot(jnp.where(low, l4, h4), 4, 0)
    return (u0, u1, u2), (r0, r1, r2), (d0, d1, d2), w


def face_slots():
    slots, at = {}, 0
    for name, comps, own, halo in (("u", 3, 5, 4), ("r", 3, 4, 3), ("d", 3, 2, 1), ("w", 1, 5, 4)):
        for c in range(comps):
            for k in range(own):
                slots[name, c, k, 0] = at
                at += 1
            for k in range(halo):
                slots[name, c, k, 1] = at
                at += 1
    return slots, at


SLOTS, N_SLOTS = face_slots()


def face_kernel(u, rhs, dif, wt, hi, lo, q_up, q_dn):
    low = sub_iota() < 4
    for out, row in ((q_up, lambda k: NB - 1 - k), (q_dn, lambda k: k)):
        for k in range(5):
            x = row(k)
            hu, hr, hd, hw = unpack(hi, lo, x, low)
            for name, own, halo in (("u", u, hu), ("r", rhs, hr), ("d", dif, hd)):
                for c in range(3):
                    if (name, c, k, 0) in SLOTS:
                        out[SLOTS[name, c, k, 0]] = own[c, x]
                    if (name, c, k, 1) in SLOTS:
                        out[SLOTS[name, c, k, 1]] = halo[c]
            out[SLOTS["w", 0, k, 0]] = wt[x]
            if ("w", 0, k, 1) in SLOTS:
                out[SLOTS["w", 0, k, 1]] = hw


def roll_y_up(pair, sub):
    a, b = rot(pair[0], -1, 0), rot(pair[1], -1, 0)
    return jnp.where(sub == 7, b, a), jnp.where(sub == 7, a, b)


def roll_y_dn(pair, sub):
    a, b = rot(pair[0], 1, 0), rot(pair[1], 1, 0)
    return jnp.where(sub == 0, b, a), jnp.where(sub == 0, a, b)


def pair_of(ref, *lead):
    return ref[(*lead, slice(0, 8))], ref[(*lead, slice(8, 16))]


def put(ref, pair, *lead):
    ref[(*lead, slice(0, 8))] = pair[0]
    ref[(*lead, slice(8, 16))] = pair[1]


def krylov_kernel(u, rhs, dif, wt, hi, lo, q_lo, q_hi, ub, r0, r1, r2, r3, v0, v1, mom, ue, we, re, de, kk):
    sub = sub_iota()
    lane = lax.broadcasted_iota(jnp.int32, (8, 128), 1)
    low = sub < 4
    zero = jnp.zeros((8, 128), F32)

    for k in range(5):
        for q, side in ((q_lo, lambda h, k: h - 1 - k), (q_hi, lambda h, k: h + NB + k)):
            for c in range(3):
                for name, ref, h in (("u", ue, 5), ("r", re, 4), ("d", de, 2)):
                    if (name, c, k, 0) in SLOTS:
                        halo = SLOTS.get((name, c, k, 1))
                        put(ref, (q[SLOTS[name, c, k, 0]], zero if halo is None else q[halo]), c, side(h, k))
            halo = SLOTS.get(("w", 0, k, 1))
            put(we, (q[SLOTS["w", 0, k, 0]], zero if halo is None else q[halo]), side(5, k))

    def fill(x, carry):
        hu, hr, hd, hw = unpack(hi, lo, x, low)
        for c in range(3):
            put(ue, (u[c, x], hu[c]), c, x + 5)
            put(re, (rhs[c, x], hr[c]), c, x + 4)
            put(de, (dif[c, x], hd[c]), c, x + 2)
        put(we, (wt[x], hw), x + 5)
        return carry

    lax.fori_loop(0, NB, fill, 0, unroll=True)

    def edges(x, ends):
        w = pair_of(we, x + 5)
        wxp, wxm = pair_of(we, x + 6), pair_of(we, x + 4)
        wyp, wym = roll_y_up(w, sub), roll_y_dn(w, sub)
        if ends is not None:
            wyp = (wyp[0], jnp.where(sub == 3, ends[0], wyp[1]))
            wym = (wym[0], jnp.where(sub == 4, ends[1], wym[1]))
        for t in range(2):
            rows = slice(8 * t, 8 * t + 8)
            inside = jnp.where(w[t] > 0.0, 0.5 * SPRING_SHEAR, 0.0)
            wzp = jnp.where(lane == 127, 0.0, rot(w[t], -1, 1))
            wzm = jnp.where(lane == 0, 0.0, rot(w[t], 1, 1))
            xp, xm, yp, ym, zp, zm = ((w[t] + o) * inside for o in (wxp[t], wxm[t], wyp[t], wym[t], wzp, wzm))
            sums = (xp + xm, yp + ym, zp + zm)
            base = (1.0 - SHIFT) + (sums[0] + sums[1] + sums[2])
            for i, val in enumerate((xp, xm, yp, ym, jnp.where(lane == 127, 0.0, zp), jnp.where(lane == 0, 0.0, zm))):
                kk[i, x + 4, rows] = val
            for c in range(3):
                kk[6 + c, x + 4, rows] = base + 1.5 * sums[c]

    def own_edges(x, carry):
        edges(x, (hi[x, 3][7:8, :], lo[x, 3][3:4, :]))
        return carry

    def far_edges(i, carry):
        edges(i - 4, None)
        edges(i + NB, None)
        return carry

    lax.fori_loop(0, 4, far_edges, 0, unroll=True)
    lax.fori_loop(0, NB, own_edges, 0, unroll=True)

    def apply_b(ref, h, x, tiles=(0, 1), ends=None):
        k = [[kk[i, x + 4, 8 * t : 8 * t + 8] if t in tiles else None for t in range(2)] for i in range(9)]
        out, mids = [], []
        for c in range(3):
            mid = pair_of(ref, c, x + h)
            yp, ym = roll_y_up(mid, sub), roll_y_dn(mid, sub)
            if ends is not None:
                yp = (yp[0], jnp.where(sub == 3, ends[0][c], yp[1]))
                ym = (ym[0], jnp.where(sub == 4, ends[1][c], ym[1]))
            res = [None, None]
            for t in tiles:
                rows = slice(8 * t, 8 * t + 8)
                sx = k[0][t] * ref[c, x + h + 1, rows] + k[1][t] * ref[c, x + h - 1, rows]
                sy = k[2][t] * yp[t] + k[3][t] * ym[t]
                sz = k[4][t] * rot(mid[t], -1, 1) + k[5][t] * rot(mid[t], 1, 1)
                res[t] = k[6 + c][t] * mid[t] - ((sx + sy) + (sz + 1.5 * (sx, sy, sz)[c]))
            out.append(res)
            mids.append(mid)
        return out, mids

    def first(x, ends, with_v):
        bu, mids = apply_b(ue, 5, x, ends=ends)
        for c in range(3):
            rh = pair_of(re, c, x + 4)
            res = [rh[t] - (bu[c][t] + SHIFT * mids[c][t]) for t in range(2)]
            put(r0, res, c, x + 4)
            if with_v:
                d = pair_of(de, c, x + 2)
                put(v0, [res[t] - d[t] for t in range(2)], c, x + 2)

    def first_own(x, carry):
        h3, l3 = hi[x, 3], lo[x, 3]
        first(x, ([h3[4 + c : 5 + c, :] for c in range(3)], [l3[c : c + 1, :] for c in range(3)]), True)
        for c in range(3):
            put(ub, pair_of(ue, c, x + 5), c, x + 1)
        return carry

    for x in (-4, -3, NB + 2, NB + 3):
        first(x, None, False)
    for x in (-2, -1, NB, NB + 1):
        first(x, None, True)
    for c in range(3):
        put(ub, pair_of(ue, c, 4), c, 0)
        put(ub, pair_of(ue, c, NB + 5), c, NB + 1)
    lax.fori_loop(0, NB, first_own, 0, unroll=True)

    def power(src, h, dst):
        def row(x, carry):
            out, _ = apply_b(src, h, x)
            for c in range(3):
                put(dst, out[c], c, x + h - 1)
            return carry

        lax.fori_loop(1 - h, NB + h - 1, row, 0, unroll=True)

    power(r0, 4, r1)
    power(v0, 2, v1)
    power(r1, 3, r2)
    power(r2, 2, r3)

    def dots(x, acc):
        r4, _ = apply_b(r3, 1, x, tiles=(0,))
        v2, _ = apply_b(v1, 1, x, tiles=(0,))
        acc = list(acc)
        for c in range(3):
            a = [ref[c, x + h, 0:8] for ref, h in ((r0, 4), (r1, 3), (r2, 2), (r3, 1))] + [r4[c][0]]
            b = [v0[c, x + 2, 0:8], v1[c, x + 1, 0:8], v2[c][0]]
            terms = [a[k // 2] * a[(k + 1) // 2] for k in range(8)]
            terms += [b[(k + 1) // 2] * a[k // 2] for k in range(5)] + [b[2] * a[3]]
            terms += [b[k // 2] * b[(k + 1) // 2] for k in range(4)]
            acc = [s + t for s, t in zip(acc, terms)] if c or True else acc
        return tuple(acc)

    acc = lax.fori_loop(0, NB, dots, (zero,) * 18, unroll=True)
    lane_row = lax.broadcasted_iota(jnp.int32, (1, 128), 1)
    line = jnp.zeros((1, 128), F32)
    for k in range(18):
        line = jnp.where(lane_row == k, jnp.sum(jnp.sum(acc[k], axis=0, keepdims=True), axis=1, keepdims=True), line)
    mom[...] = jnp.broadcast_to(line, mom.shape)


def two_iterations(m):
    alpha = m[0] / (SHIFT * m[0] + m[1])
    p0, p1 = 1.0 - SHIFT * alpha, -alpha
    new = p0 * p0 * m[0] + 2.0 * p0 * p1 * m[1] + p1 * p1 * m[2]
    e0, e1 = p0 + new / m[0], p1
    d0 = e0 * e0 * m[0] + 2.0 * e0 * e1 * m[1] + e1 * e1 * m[2]
    d1 = e0 * e0 * m[1] + 2.0 * e0 * e1 * m[2] + e1 * e1 * m[3]
    again = new / (SHIFT * d0 + d1)
    return alpha + again * e0, again * e1


def product3(value, table):
    high, rest = split(value)
    dot = lambda a, b: jnp.dot(a, b, preferred_element_type=F32)
    return dot(high, table[0]) + (dot(rest, table[0]) + dot(high, table[1]))


def code_kernel(ub, r0, r1, r2, r3, v0, v1, mom, car, mix, tz, disp, code, uf, fl):
    sub = sub_iota()
    lane = lax.broadcasted_iota(jnp.int32, (8, 128), 1)
    total = jnp.sum(mom[...], axis=0, keepdims=True)
    lane_row = lax.broadcasted_iota(jnp.int32, (1, 128), 1)
    m = [jnp.sum(jnp.where(lane_row == k, total, 0.0), axis=1, keepdims=True) for k in range(18)]
    rr, vr, vv = m[:8], m[8:14], m[14:]
    a0, a1 = two_iterations(rr)
    g = (a0 * (2.0 - SHIFT), a1 * (2.0 - SHIFT) - a0, -a1)
    mix2 = []
    for k in range(4):
        s = vv[k]
        for i in range(3):
            s = s + 2.0 * g[i] * vr[k + i]
            for j in range(3):
                s = s + g[i] * g[j] * rr[k + i + j]
        mix2.append(s)
    b0, b1 = two_iterations(mix2)
    coef = [b0, b1, a0 + b0 * g[0], a1 + b0 * g[1] + b1 * g[0], b0 * g[2] + b1 * g[1], b1 * g[2]]
    coef = [jnp.broadcast_to(v, (8, 128)) for v in coef]
    parts = ((v0, 2), (v1, 1), (r0, 4), (r1, 3), (r2, 2), (r3, 1))

    def combine(i, carry):
        for c in range(3):
            for t in range(2):
                rows = slice(8 * t, 8 * t + 8)
                s = ub[c, i, rows]
                for w, (ref, h) in zip(coef, parts):
                    s = s + w * ref[c, i + h - 1, rows]
                uf[c, i, rows] = s
        return carry

    lax.fori_loop(0, NB + 2, combine, 0, unroll=True)

    def stress(x, carry):
        k = car[x]
        for c in range(3):
            own = uf[c, x + 1, 0:8]
            disp[c, x] = own
            fl[c, x] = own
        fl[3, x] = k * (uf[0, x + 2, 0:8] - uf[0, x, 0:8])
        y = pair_of(uf, 1, x + 1)
        fl[4, x] = k * (roll_y_up(y, sub)[0] - roll_y_dn(y, sub)[0])
        z = uf[2, x + 1, 0:8]
        fl[5, x] = k * (jnp.where(lane == 127, 0.0, rot(z, -1, 1)) - jnp.where(lane == 0, 0.0, rot(z, 1, 1)))
        return carry

    lax.fori_loop(0, NB, stress, 0, unroll=True)
    along_z = product3(fl[...].reshape(768, 128), tz)
    turned = jnp.concatenate([along_z[128 * ch : 128 * ch + 128].T for ch in range(6)], axis=0)
    done = product3(turned, mix)
    for ch in range(6):
        for i in range(16):
            code[pl.ds(48 * i + ch, 8, stride=6), :] = done[128 * ch + 8 * i : 128 * ch + 8 * i + 8]


def wavelet_kernel(got, w1, w2, w3, out, xs):
    sub = sub_iota()
    lane = lax.broadcasted_iota(jnp.int32, (8, 128), 1)
    for j in range(16):
        tiles = []
        for ch in range(6):
            tile = got[pl.ds(48 * j + ch, 8, stride=6), :]
            for b in range(3):
                step = 1 << b
                s_bit, l_bit = (sub // step) % 2, (lane // step) % 2
                up, down = rot(rot(tile, -step, 0), step, 1), rot(rot(tile, step, 0), -step, 1)
                tile = jnp.where(s_bit == l_bit, tile, jnp.where(s_bit == 0, up, down))
            tiles.append(tile)
        high, rest = split(jnp.concatenate(tiles, axis=0))
        xs[0, j] = high
        xs[1, j] = rest

    def product(first, step, count, weight):
        rows = [
            jnp.concatenate([xs[part, (first + step * q + t) % 16] for t in range(count)], axis=1)
            for part in range(2)
            for q in range(16 // step)
        ]
        both = jnp.dot(jnp.concatenate(rows, axis=0), weight[...], preferred_element_type=F32)
        half = both.shape[0] // 2
        return both[:half] + both[half:]

    def emit(value, tile):
        for ch in range(6):
            out[pl.ds(128 * ch + tile, 8, stride=16), :] = value[8 * ch : 8 * ch + 8]

    fine = product(0, 2, 3, w1)
    for q in range(8):
        emit(fine[48 * q : 48 * q + 48], 8 + q)
    middle = product(15, 4, 6, w2)
    for q in range(4):
        emit(middle[48 * q : 48 * q + 48], 4 + q)
    coarse = product(15, 8, 10, w3)
    for q in range(2):
        emit(coarse[48 * q : 48 * q + 48, :128], q)
        emit(coarse[48 * q : 48 * q + 48, 128:], 2 + q)


def call(kernel, outs, scratch=(), **specs):
    return pl.pallas_call(
        kernel,
        out_shape=[jax.ShapeDtypeStruct(s, F32) for s in outs],
        scratch_shapes=[pltpu.VMEM(s, F32) if isinstance(s, tuple) else s for s in scratch],
        **specs,
        compiler_params=pltpu.CompilerParams(vmem_limit_bytes=40 * 2**20),
    )


def body(u_now, u_prev, force, stiffness, broken, flags):
    n_slab, n_grp = lax.axis_size("slab"), lax.axis_size("grp")
    total = n_slab * n_grp
    block, one = (3, NB, 8, 128), (NB, 8, 128)
    m_up, m_dn, rhs, dif, wt, car, u_here = call(
        pack_kernel,
        [(NB, 5, 8, 128)] * 2 + [block, block, one, one, block],
        [block, block, one, pltpu.VMEM(broken.shape, jnp.int32), pltpu.VMEM(flags.shape, jnp.int32), pltpu.SemaphoreType.DMA((6,))],
        in_specs=[pl.BlockSpec(memory_space=pltpu.HBM)] * 6,
    )(*(pltpu.with_memory_space_constraint(v, pltpu.HBM) for v in (u_now, u_prev, force, stiffness, broken, flags)))
    up = lambda n: [(i, i + 1) for i in range(n - 1)]
    down = lambda n: [(i + 1, i) for i in range(n - 1)]
    lo = lax.ppermute(m_up, "grp", up(n_grp))
    hi = lax.ppermute(m_dn, "grp", down(n_grp))
    q_up, q_dn = call(face_kernel, [(N_SLOTS, 8, 128)] * 2)(u_here, rhs, dif, wt, hi, lo)
    q_lo = lax.ppermute(q_up, "slab", up(n_slab))
    q_hi = lax.ppermute(q_dn, "slab", down(n_slab))
    wide = lambda h: (3, NB + 2 * h, 16, 128)
    *basis, mom = call(
        krylov_kernel,
        [wide(1), wide(4), wide(3), wide(2), wide(1), wide(2), wide(1), (total, 128)],
        [wide(5), wide(5)[1:], wide(4), wide(2), (9, NB + 8, 16, 128)],
    )(u_here, rhs, dif, wt, hi, lo, q_lo, q_hi)
    mom = lax.all_to_all(mom.reshape(total, 1, 128), ("slab", "grp"), 0, 0, tiled=True).reshape(total, 128)
    table = cosine_table()
    mix = two_parts(np.kron(np.kron(np.eye(4), table), np.kron(np.eye(2), table)).T)
    tz = two_parts(np.kron(np.eye(32), table).T)
    disp, code = call(
        code_kernel, [block, (768, 128)], [wide(1), (6, NB, 8, 128)]
    )(*basis, mom, car, mix, tz)
    got = lax.all_to_all(code.reshape(n_slab, 1, 768), "slab", 0, 0, tiled=True).reshape(768, 128)
    (coeffs,) = call(wavelet_kernel, [(768, 128)], [pltpu.VMEM((2, 16, 48, 128), BF16)])(got, *(jnp.asarray(w, BF16) for w in wavelet_tables()))
    return (disp, coeffs.reshape(6, 8, 1, 2048))


def solution(mesh):
    return jax.shard_map(
        body,
        mesh=mesh,
        in_specs=(
            P(None, "slab", "grp", None),
            P(None, "slab", "grp", None),
            P(None, "slab", "grp", None),
            P("slab", "grp", None),
            P("slab", "grp", None),
            P("slab", "grp", None),
        ),
        out_specs=(P(None, "slab", "grp", None), P(None, "grp", "slab", None)),
        check_vma=False,
    )
```

```python
import jax
import jax.numpy as jnp
import numpy as np
from jax import lax
from jax.experimental import pallas as pl
from jax.experimental.pallas import tpu as pltpu
from jax.sharding import PartitionSpec as P

SPRING_SHEAR = 0.4
CRACK_CUT = 0.9
SHIFT = 2.5
F32 = jnp.float32
BF16 = jnp.bfloat16
NB = 16


def cosine_table():
    freq = np.arange(4)[:, None]
    place = np.arange(4)[None, :]
    factor = np.where(freq == 0, 0.5, np.sqrt(0.5))
    return factor * np.cos(np.pi * (2 * place + 1) * freq / 8.0)


def lift_np(signal):
    even, odd = signal[..., 0::2], signal[..., 1::2]
    detail = odd - 0.5 * (even + np.roll(even, -1, axis=-1))
    approx = even + 0.25 * (np.roll(detail, 1, axis=-1) + detail)
    return approx, detail


def wavelet_tables():
    size = 2048
    eye = np.eye(size)
    a1, d1 = lift_np(eye)
    a2, d2 = lift_np(a1)
    a3, d3 = lift_np(a2)
    lane = np.arange(128)
    place = (lane % 8) * 16 + lane // 8

    def rows(first, count):
        return np.concatenate([((first + t) % 16) * 128 + place for t in range(count)])

    w1 = d1[rows(0, 3)][:, :128]
    w2 = d2[rows(3, 6)][:, 128:256]
    w3 = np.concatenate([a3[rows(7, 10)][:, 128:], d3[rows(7, 10)][:, 128:]], axis=1)
    return [np.asarray(w, np.float32) for w in (w1, w2, w3)]


def two_parts(table):
    high = np.asarray(table, BF16)
    return jnp.stack([jnp.asarray(high), jnp.asarray(np.asarray(table - high.astype(np.float64), BF16))])


def sub_iota():
    return lax.broadcasted_iota(jnp.int32, (8, 128), 0)


def split(value):
    high = value.astype(BF16)
    return high, (value - high.astype(F32)).astype(BF16)


def rot(tile, shift, axis):
    return pltpu.roll(tile, shift % tile.shape[axis], axis)


def is_even(axis):
    return lax.axis_index(axis) % 2 == 0


def pack_kernel(u_in, up_in, f_in, st_in, br_in, fl_in, m_near, m_far, q_near, q_far, rhs, dif, wt, car, u, up, f, st, br, fl, sems):
    pairs = ((br_in, br), (fl_in, fl), (st_in, st), (u_in, u), (up_in, up), (f_in, f))
    copies = [pltpu.make_async_copy(a, b, sems.at[i]) for i, (a, b) in enumerate(pairs)]
    for copy in copies:
        copy.start()
    for copy in copies:
        copy.wait()
    sub = sub_iota()
    low = sub < 4
    even, even_x = is_even("grp"), is_even("slab")
    spread = (
        lax.broadcasted_iota(jnp.int32, (32, 128), 1) // 4
        == lax.broadcasted_iota(jnp.int32, (32, 128), 0)
    ).astype(F32)
    held = []
    for p in range(4):
        wide_b = jnp.dot(br[p].astype(F32), spread, preferred_element_type=F32)
        wide_f = jnp.dot(fl[p].astype(F32), spread, preferred_element_type=F32)
        cut = 1.0 - CRACK_CUT * jnp.where(low, wide_b[0:1, :], wide_b[1:2, :])
        on = jnp.where(low, wide_f[0:1, :], wide_f[1:2, :])
        for x in range(4 * p, 4 * p + 4):
            w = st[x] * cut
            wt[x] = w
            car[x] = 0.5 * on * w
            uu, rr, dd, to_up, to_dn = [], [], [], [], []
            for c in range(3):
                a = u[c, x]
                b = up[c, x]
                uu.append(a)
                rr.append((2.0 * a - b) + f[c, x])
                dd.append(a - b)
                rhs[c, x] = rr[c]
                dif[c, x] = dd[c]
            u1, w4, r1 = rot(uu[1], 4, 0), rot(w, 4, 0), rot(rr[1], 4, 0)
            to_up.append(jnp.where(low, u1, uu[0]))
            to_up.append(jnp.where(low, w4, uu[2]))
            to_up.append(jnp.where(low, r1, rr[0]))
            extra = jnp.where(sub == 0, rot(uu[0], -3, 0), jnp.where(sub == 1, rot(uu[1], -2, 0), jnp.where(sub == 2, rot(uu[2], -1, 0), w)))
            to_up.append(jnp.where(low, extra, rr[2]))
            to_up.append(jnp.where(sub >= 6, dd[0], jnp.where(sub >= 4, rot(dd[1], -2, 0), rot(dd[2], 4, 0))))
            to_dn.append(jnp.where(low, uu[0], u1))
            to_dn.append(jnp.where(low, uu[2], w4))
            to_dn.append(jnp.where(low, rr[0], r1))
            extra = jnp.where(sub == 4, uu[0], jnp.where(sub == 5, rot(uu[1], 1, 0), jnp.where(sub == 6, rot(uu[2], 2, 0), rot(w, 3, 0))))
            to_dn.append(jnp.where(low, rr[2], extra))
            to_dn.append(jnp.where(sub < 2, dd[0], jnp.where(sub < 4, rot(dd[1], 2, 0), rot(dd[2], 4, 0))))
            for t in range(5):
                m_near[x, t] = jnp.where(even, to_up[t], to_dn[t])
                m_far[x, t] = jnp.where(even, to_dn[t], to_up[t])
            held.append([(name, c, tile) for name, own in (("u", uu), ("r", rr), ("d", dd), ("w", [w])) for c, tile in enumerate(own)])
    for k in range(5):
        for (name, c, to_dn), (_, _, to_up) in zip(held[k], held[NB - 1 - k]):
            if (name, c, k) in OWN:
                q_near[OWN[name, c, k]] = jnp.where(even_x, to_up, to_dn)
                q_far[OWN[name, c, k]] = jnp.where(even_x, to_dn, to_up)


def unpack(near, far, x, low, even):
    h0, h1, h2, h3, h4 = (jnp.where(even, near[x, t], far[x, t]) for t in range(5))
    l0, l1, l2, l3, l4 = (jnp.where(even, far[x, t], near[x, t]) for t in range(5))
    u0 = jnp.where(low, h0, l0)
    u1 = rot(jnp.where(low, l0, h0), 4, 0)
    u2 = jnp.where(low, h1, l1)
    w = rot(jnp.where(low, l1, h1), 4, 0)
    r0 = jnp.where(low, h2, l2)
    r1 = rot(jnp.where(low, l2, h2), 4, 0)
    r2 = jnp.where(low, h3, l3)
    d0 = jnp.where(low, h4, l4)
    d1 = jnp.where(low, rot(h4, -2, 0), rot(l4, 2, 0))
    d2 = rot(jnp.where(low, l4, h4), 4, 0)
    return (u0, u1, u2), (r0, r1, r2), (d0, d1, d2), w


def face_slots(part):
    slots, at = {}, 0
    for name, comps, deep in (("u", 3, (5, 4)), ("r", 3, (4, 3)), ("d", 3, (2, 1)), ("w", 1, (5, 4))):
        for c in range(comps):
            for k in range(deep[part]):
                slots[name, c, k] = at
                at += 1
    return slots


OWN, HALO = face_slots(0), face_slots(1)


def corner_kernel(near, far, c_near, c_far):
    low = sub_iota() < 4
    even_y, even_x = is_even("grp"), is_even("slab")

    def tiles(k, x):
        hu, hr, hd, hw = unpack(near, far, x, low, even_y)
        out = {(name, c, k): halo[c] for name, halo in (("u", hu), ("r", hr), ("d", hd)) for c in range(3)}
        out["w", 0, k] = hw
        return out

    for k in range(4):
        to_up, to_dn = tiles(k, NB - 1 - k), tiles(k, k)
        for key in to_up:
            if key in HALO:
                c_near[HALO[key]] = jnp.where(even_x, to_up[key], to_dn[key])
                c_far[HALO[key]] = jnp.where(even_x, to_dn[key], to_up[key])


def roll_y_up(pair, sub):
    a, b = rot(pair[0], -1, 0), rot(pair[1], -1, 0)
    return jnp.where(sub == 7, b, a), jnp.where(sub == 7, a, b)


def roll_y_dn(pair, sub):
    a, b = rot(pair[0], 1, 0), rot(pair[1], 1, 0)
    return jnp.where(sub == 0, b, a), jnp.where(sub == 0, a, b)


def pair_of(ref, *lead):
    return ref[(*lead, slice(0, 8))], ref[(*lead, slice(8, 16))]


def put(ref, pair, *lead):
    ref[(*lead, slice(0, 8))] = pair[0]
    ref[(*lead, slice(8, 16))] = pair[1]


def krylov_kernel(u, rhs, dif, wt, near, far, q_near, q_far, c_near, c_far, ub, r0, r1, r2, r3, v0, v1, mom, ue, we, re, de, kk):
    even_y, even_x = is_even("grp"), is_even("slab")
    sub = sub_iota()
    lane = lax.broadcasted_iota(jnp.int32, (8, 128), 1)
    low = sub < 4
    zero = jnp.zeros((8, 128), F32)

    def faces(a, b):
        return jnp.where(even_x, b, a), jnp.where(even_x, a, b)

    for k in range(5):
        for name, ref, h, lead in (("u", ue, 5, range(3)), ("r", re, 4, range(3)), ("d", de, 2, range(3)), ("w", we, 5, (None,))):
            for c in lead:
                key = (name, c or 0, k)
                if key in OWN:
                    own = faces(q_near[OWN[key]], q_far[OWN[key]])
                    halo = faces(c_near[HALO[key]], c_far[HALO[key]]) if key in HALO else (zero, zero)
                    where = () if c is None else (c,)
                    put(ref, (own[0], halo[0]), *where, h - 1 - k)
                    put(ref, (own[1], halo[1]), *where, h + NB + k)

    def fill(x, carry):
        hu, hr, hd, hw = unpack(near, far, x, low, even_y)
        for c in range(3):
            put(ue, (u[c, x], hu[c]), c, x + 5)
            put(re, (rhs[c, x], hr[c]), c, x + 4)
            put(de, (dif[c, x], hd[c]), c, x + 2)
        put(we, (wt[x], hw), x + 5)
        return carry

    lax.fori_loop(0, NB, fill, 0, unroll=True)

    def edges(x, ends):
        w = pair_of(we, x + 5)
        wxp, wxm = pair_of(we, x + 6), pair_of(we, x + 4)
        wyp, wym = roll_y_up(w, sub), roll_y_dn(w, sub)
        if ends is not None:
            wyp = (wyp[0], jnp.where(sub == 3, ends[0], wyp[1]))
            wym = (wym[0], jnp.where(sub == 4, ends[1], wym[1]))
        for t in range(2):
            rows = slice(8 * t, 8 * t + 8)
            inside = jnp.where(w[t] > 0.0, 0.5 * SPRING_SHEAR, 0.0)
            wzp = jnp.where(lane == 127, 0.0, rot(w[t], -1, 1))
            wzm = jnp.where(lane == 0, 0.0, rot(w[t], 1, 1))
            xp, xm, yp, ym, zp, zm = ((w[t] + o) * inside for o in (wxp[t], wxm[t], wyp[t], wym[t], wzp, wzm))
            sums = (xp + xm, yp + ym, zp + zm)
            base = (1.0 - SHIFT) + (sums[0] + sums[1] + sums[2])
            for i, val in enumerate((xp, xm, yp, ym, jnp.where(lane == 127, 0.0, zp), jnp.where(lane == 0, 0.0, zm))):
                kk[i, x + 4, rows] = val
            for c in range(3):
                kk[6 + c, x + 4, rows] = base + 1.5 * sums[c]

    def extra_rows(x):
        a, b = near[x, 3], far[x, 3]
        return jnp.where(even_y, a, b), jnp.where(even_y, b, a)

    def own_edges(x, carry):
        h3, l3 = extra_rows(x)
        edges(x, (h3[7:8, :], l3[3:4, :]))
        return carry

    def far_edges(i, carry):
        edges(i - 4, None)
        edges(i + NB, None)
        return carry

    lax.fori_loop(0, 4, far_edges, 0, unroll=True)
    lax.fori_loop(0, NB, own_edges, 0, unroll=True)

    def apply_b(ref, h, x, tiles=(0, 1), ends=None):
        k = [[kk[i, x + 4, 8 * t : 8 * t + 8] if t in tiles else None for t in range(2)] for i in range(9)]
        out, mids = [], []
        for c in range(3):
            mid = pair_of(ref, c, x + h)
            yp, ym = roll_y_up(mid, sub), roll_y_dn(mid, sub)
            if ends is not None:
                yp = (yp[0], jnp.where(sub == 3, ends[0][c], yp[1]))
                ym = (ym[0], jnp.where(sub == 4, ends[1][c], ym[1]))
            res = [None, None]
            for t in tiles:
                rows = slice(8 * t, 8 * t + 8)
                sx = k[0][t] * ref[c, x + h + 1, rows] + k[1][t] * ref[c, x + h - 1, rows]
                sy = k[2][t] * yp[t] + k[3][t] * ym[t]
                sz = k[4][t] * rot(mid[t], -1, 1) + k[5][t] * rot(mid[t], 1, 1)
                res[t] = k[6 + c][t] * mid[t] - ((sx + sy) + (sz + 1.5 * (sx, sy, sz)[c]))
            out.append(res)
            mids.append(mid)
        return out, mids

    def first(x, ends, with_v):
        bu, mids = apply_b(ue, 5, x, ends=ends)
        for c in range(3):
            rh = pair_of(re, c, x + 4)
            res = [rh[t] - (bu[c][t] + SHIFT * mids[c][t]) for t in range(2)]
            put(r0, res, c, x + 4)
            if with_v:
                d = pair_of(de, c, x + 2)
                put(v0, [res[t] - d[t] for t in range(2)], c, x + 2)

    def first_own(x, carry):
        h3, l3 = extra_rows(x)
        first(x, ([h3[4 + c : 5 + c, :] for c in range(3)], [l3[c : c + 1, :] for c in range(3)]), True)
        for c in range(3):
            put(ub, pair_of(ue, c, x + 5), c, x + 1)
        return carry

    for x in (-4, -3, NB + 2, NB + 3):
        first(x, None, False)
    for x in (-2, -1, NB, NB + 1):
        first(x, None, True)
    for c in range(3):
        put(ub, pair_of(ue, c, 4), c, 0)
        put(ub, pair_of(ue, c, NB + 5), c, NB + 1)
    lax.fori_loop(0, NB, first_own, 0, unroll=True)

    def power(src, h, dst):
        def row(x, carry):
            out, _ = apply_b(src, h, x)
            for c in range(3):
                put(dst, out[c], c, x + h - 1)
            return carry

        lax.fori_loop(1 - h, NB + h - 1, row, 0, unroll=True)

    power(r0, 4, r1)
    power(v0, 2, v1)
    power(r1, 3, r2)
    power(r2, 2, r3)

    def dots(x, acc):
        r4, _ = apply_b(r3, 1, x, tiles=(0,))
        v2, _ = apply_b(v1, 1, x, tiles=(0,))
        acc = list(acc)
        for c in range(3):
            a = [ref[c, x + h, 0:8] for ref, h in ((r0, 4), (r1, 3), (r2, 2), (r3, 1))] + [r4[c][0]]
            b = [v0[c, x + 2, 0:8], v1[c, x + 1, 0:8], v2[c][0]]
            terms = [a[k // 2] * a[(k + 1) // 2] for k in range(8)]
            terms += [b[(k + 1) // 2] * a[k // 2] for k in range(5)] + [b[2] * a[3]]
            terms += [b[k // 2] * b[(k + 1) // 2] for k in range(4)]
            acc = [s + t for s, t in zip(acc, terms)] if c or True else acc
        return tuple(acc)

    acc = lax.fori_loop(0, NB, dots, (zero,) * 18, unroll=True)
    lane_row = lax.broadcasted_iota(jnp.int32, (1, 128), 1)
    line = jnp.zeros((1, 128), F32)
    for k in range(18):
        line = jnp.where(lane_row == k, jnp.sum(jnp.sum(acc[k], axis=0, keepdims=True), axis=1, keepdims=True), line)
    mom[...] = jnp.broadcast_to(line, mom.shape)


def two_iterations(m):
    alpha = m[0] / (SHIFT * m[0] + m[1])
    p0, p1 = 1.0 - SHIFT * alpha, -alpha
    new = p0 * p0 * m[0] + 2.0 * p0 * p1 * m[1] + p1 * p1 * m[2]
    e0, e1 = p0 + new / m[0], p1
    d0 = e0 * e0 * m[0] + 2.0 * e0 * e1 * m[1] + e1 * e1 * m[2]
    d1 = e0 * e0 * m[1] + 2.0 * e0 * e1 * m[2] + e1 * e1 * m[3]
    again = new / (SHIFT * d0 + d1)
    return alpha + again * e0, again * e1


def product3(value, table):
    high, rest = split(value)
    dot = lambda a, b: jnp.dot(a, b, preferred_element_type=F32)
    return dot(high, table[0]) + (dot(rest, table[0]) + dot(high, table[1]))


def code_kernel(ub, r0, r1, r2, r3, v0, v1, mom, car, mix, tz, disp, code, uf, fl):
    sub = sub_iota()
    lane = lax.broadcasted_iota(jnp.int32, (8, 128), 1)
    total = jnp.sum(mom[...], axis=0, keepdims=True)
    lane_row = lax.broadcasted_iota(jnp.int32, (1, 128), 1)
    m = [jnp.sum(jnp.where(lane_row == k, total, 0.0), axis=1, keepdims=True) for k in range(18)]
    rr, vr, vv = m[:8], m[8:14], m[14:]
    a0, a1 = two_iterations(rr)
    g = (a0 * (2.0 - SHIFT), a1 * (2.0 - SHIFT) - a0, -a1)
    mix2 = []
    for k in range(4):
        s = vv[k]
        for i in range(3):
            s = s + 2.0 * g[i] * vr[k + i]
            for j in range(3):
                s = s + g[i] * g[j] * rr[k + i + j]
        mix2.append(s)
    b0, b1 = two_iterations(mix2)
    coef = [b0, b1, a0 + b0 * g[0], a1 + b0 * g[1] + b1 * g[0], b0 * g[2] + b1 * g[1], b1 * g[2]]
    coef = [jnp.broadcast_to(v, (8, 128)) for v in coef]
    parts = ((v0, 2), (v1, 1), (r0, 4), (r1, 3), (r2, 2), (r3, 1))

    def combine(i, carry):
        for c in range(3):
            for t in range(2):
                rows = slice(8 * t, 8 * t + 8)
                s = ub[c, i, rows]
                for w, (ref, h) in zip(coef, parts):
                    s = s + w * ref[c, i + h - 1, rows]
                uf[c, i, rows] = s
        return carry

    lax.fori_loop(0, NB + 2, combine, 0, unroll=True)

    def stress(x, carry):
        k = car[x]
        for c in range(3):
            own = uf[c, x + 1, 0:8]
            disp[c, x] = own
            fl[c, x] = own
        fl[3, x] = k * (uf[0, x + 2, 0:8] - uf[0, x, 0:8])
        y = pair_of(uf, 1, x + 1)
        fl[4, x] = k * (roll_y_up(y, sub)[0] - roll_y_dn(y, sub)[0])
        z = uf[2, x + 1, 0:8]
        fl[5, x] = k * (jnp.where(lane == 127, 0.0, rot(z, -1, 1)) - jnp.where(lane == 0, 0.0, rot(z, 1, 1)))
        return carry

    lax.fori_loop(0, NB, stress, 0, unroll=True)
    along_z = product3(fl[...].reshape(768, 128), tz)
    turned = jnp.concatenate([along_z[128 * ch : 128 * ch + 128].T for ch in range(6)], axis=0)
    done = product3(turned, mix)
    for ch in range(6):
        for i in range(16):
            code[pl.ds(48 * i + ch, 8, stride=6), :] = done[128 * ch + 8 * i : 128 * ch + 8 * i + 8]


def wavelet_kernel(got, w1, w2, w3, out, xs):
    sub = sub_iota()
    lane = lax.broadcasted_iota(jnp.int32, (8, 128), 1)
    for j in range(16):
        tiles = []
        for ch in range(6):
            tile = got[pl.ds(48 * j + ch, 8, stride=6), :]
            for b in range(3):
                step = 1 << b
                s_bit, l_bit = (sub // step) % 2, (lane // step) % 2
                up, down = rot(rot(tile, -step, 0), step, 1), rot(rot(tile, step, 0), -step, 1)
                tile = jnp.where(s_bit == l_bit, tile, jnp.where(s_bit == 0, up, down))
            tiles.append(tile)
        high, rest = split(jnp.concatenate(tiles, axis=0))
        xs[0, j] = high
        xs[1, j] = rest

    def product(first, step, count, weight):
        rows = [
            jnp.concatenate([xs[part, (first + step * q + t) % 16] for t in range(count)], axis=1)
            for part in range(2)
            for q in range(16 // step)
        ]
        both = jnp.dot(jnp.concatenate(rows, axis=0), weight[...], preferred_element_type=F32)
        half = both.shape[0] // 2
        return both[:half] + both[half:]

    def emit(value, tile):
        for ch in range(6):
            out[pl.ds(128 * ch + tile, 8, stride=16), :] = value[8 * ch : 8 * ch + 8]

    fine = product(0, 2, 3, w1)
    for q in range(8):
        emit(fine[48 * q : 48 * q + 48], 8 + q)
    middle = product(15, 4, 6, w2)
    for q in range(4):
        emit(middle[48 * q : 48 * q + 48], 4 + q)
    coarse = product(15, 8, 10, w3)
    for q in range(2):
        emit(coarse[48 * q : 48 * q + 48, :128], q)
        emit(coarse[48 * q : 48 * q + 48, 128:], 2 + q)


def call(kernel, outs, scratch=(), **specs):
    return pl.pallas_call(
        kernel,
        out_shape=[jax.ShapeDtypeStruct(s, F32) for s in outs],
        scratch_shapes=[pltpu.VMEM(s, F32) if isinstance(s, tuple) else s for s in scratch],
        **specs,
        compiler_params=pltpu.CompilerParams(vmem_limit_bytes=40 * 2**20),
    )


def swap(near, far, axis, count):
    both = lambda first: [p for i in range(first, count - 1, 2) for p in ((i, i + 1), (i + 1, i))]
    return lax.ppermute(near, axis, both(0)), lax.ppermute(far, axis, both(1))


def share(rows, axes, groups):
    count = len(groups[0])
    return lax.all_to_all(rows.reshape(count, 1, 128), axes, 0, 0, axis_index_groups=groups, tiled=True).reshape(count, 128)


def total_kernel(rows, out):
    out[...] = jnp.broadcast_to(jnp.sum(rows[...], axis=0, keepdims=True), out.shape)


def body(u_now, u_prev, force, stiffness, broken, flags):
    n_slab, n_grp = lax.axis_size("slab"), lax.axis_size("grp")
    planes = [[16 * y + k for k in range(16)] for y in range(n_slab // 16)]
    lines = [[(16 * y + k) * n_grp + g for y in range(n_slab // 16) for g in range(n_grp)] for k in range(16)]
    block, one = (3, NB, 8, 128), (NB, 8, 128)
    m_near, m_far, q_near, q_far, rhs, dif, wt, car, u_here = call(
        pack_kernel,
        [(NB, 5, 8, 128)] * 2 + [(len(OWN), 8, 128)] * 2 + [block, block, one, one, block],
        [block, block, one, pltpu.VMEM(broken.shape, jnp.int32), pltpu.VMEM(flags.shape, jnp.int32), pltpu.SemaphoreType.DMA((6,))],
        in_specs=[pl.BlockSpec(memory_space=pltpu.HBM)] * 6,
    )(*(pltpu.with_memory_space_constraint(v, pltpu.HBM) for v in (u_now, u_prev, force, stiffness, broken, flags)))
    m_near, m_far = swap(m_near, m_far, "grp", n_grp)
    q_near, q_far = swap(q_near, q_far, "slab", n_slab)
    c_near, c_far = call(corner_kernel, [(len(HALO), 8, 128)] * 2)(m_near, m_far)
    c_near, c_far = swap(c_near, c_far, "slab", n_slab)
    wide = lambda h: (3, NB + 2 * h, 16, 128)
    *basis, mom = call(
        krylov_kernel,
        [wide(1), wide(4), wide(3), wide(2), wide(1), wide(2), wide(1), (len(lines[0]), 128)],
        [wide(5), wide(5)[1:], wide(4), wide(2), (9, NB + 8, 16, 128)],
    )(u_here, rhs, dif, wt, m_near, m_far, q_near, q_far, c_near, c_far)
    mom = share(mom, ("slab", "grp"), lines)
    (mom,) = call(total_kernel, [(len(planes[0]), 128)])(mom)
    mom = share(mom, "slab", planes)
    table = cosine_table()
    mix = two_parts(np.kron(np.kron(np.eye(4), table), np.kron(np.eye(2), table)).T)
    tz = two_parts(np.kron(np.eye(32), table).T)
    disp, code = call(
        code_kernel, [block, (768, 128)], [wide(1), (6, NB, 8, 128)]
    )(*basis, mom, car, mix, tz)
    got = lax.all_to_all(code.reshape(n_slab, 1, 768), "slab", 0, 0, tiled=True).reshape(768, 128)
    (coeffs,) = call(wavelet_kernel, [(768, 128)], [pltpu.VMEM((2, 16, 48, 128), BF16)])(got, *(jnp.asarray(w, BF16) for w in wavelet_tables()))
    return (disp, coeffs.reshape(6, 8, 1, 2048))


def solution(mesh):
    return jax.shard_map(
        body,
        mesh=mesh,
        in_specs=(
            P(None, "slab", "grp", None),
            P(None, "slab", "grp", None),
            P(None, "slab", "grp", None),
            P("slab", "grp", None),
            P("slab", "grp", None),
            P("slab", "grp", None),
        ),
        out_specs=(P(None, "slab", "grp", None), P(None, "grp", "slab", None)),
        check_vma=False,
    )
```

```python
import jax
import jax.numpy as jnp
import numpy as np
from jax import lax
from jax.experimental import pallas as pl
from jax.experimental.pallas import tpu as pltpu
from jax.sharding import PartitionSpec as P

SPRING_SHEAR = 0.4
CRACK_CUT = 0.9
SHIFT = 2.5
F32 = jnp.float32
BF16 = jnp.bfloat16
NB = 16


def cosine_table():
    freq = np.arange(4)[:, None]
    place = np.arange(4)[None, :]
    factor = np.where(freq == 0, 0.5, np.sqrt(0.5))
    return factor * np.cos(np.pi * (2 * place + 1) * freq / 8.0)


def lift_np(signal):
    even, odd = signal[..., 0::2], signal[..., 1::2]
    detail = odd - 0.5 * (even + np.roll(even, -1, axis=-1))
    approx = even + 0.25 * (np.roll(detail, 1, axis=-1) + detail)
    return approx, detail


def wavelet_tables():
    size = 2048
    eye = np.eye(size)
    a1, d1 = lift_np(eye)
    a2, d2 = lift_np(a1)
    a3, d3 = lift_np(a2)
    lane = np.arange(128)
    place = (lane % 8) * 16 + lane // 8

    def rows(first, count):
        return np.concatenate([((first + t) % 16) * 128 + place for t in range(count)])

    w1 = d1[rows(0, 3)][:, :128]
    w2 = d2[rows(3, 6)][:, 128:256]
    w3 = np.concatenate([a3[rows(7, 10)][:, 128:], d3[rows(7, 10)][:, 128:]], axis=1)
    return [np.asarray(w, np.float32) for w in (w1, w2, w3)]


def two_parts(table):
    high = np.asarray(table, BF16)
    return jnp.stack([jnp.asarray(high), jnp.asarray(np.asarray(table - high.astype(np.float64), BF16))])


def sub_iota():
    return lax.broadcasted_iota(jnp.int32, (8, 128), 0)


def split(value):
    high = value.astype(BF16)
    return high, (value - high.astype(F32)).astype(BF16)


def rot(tile, shift, axis):
    return pltpu.roll(tile, shift % tile.shape[axis], axis)


def pick(x, outer, inner):
    if 4 <= x < NB - 4:
        return inner, x - 4
    return outer, x if x < 4 else x - 8


def is_even(axis):
    return lax.axis_index(axis) % 2 == 0


def pack_kernel(u_in, up_in, f_in, st_in, br_in, fl_in, m_near, m_far, n_near, n_far, rhs, dif, wt, car, u, up, f, st, br, fl, sems):
    pairs = ((br_in, br), (fl_in, fl), (st_in, st), (u_in, u), (up_in, up), (f_in, f))
    copies = [pltpu.make_async_copy(a, b, sems.at[i]) for i, (a, b) in enumerate(pairs)]
    for copy in copies:
        copy.start()
    for copy in copies:
        copy.wait()
    sub = sub_iota()
    low = sub < 4
    even = is_even("grp")
    n_near[:, 5:] = jnp.zeros((NB // 2, 4, 8, 128), F32)
    n_far[:, 5:] = jnp.zeros((NB // 2, 4, 8, 128), F32)
    spread = (
        lax.broadcasted_iota(jnp.int32, (32, 128), 1) // 4
        == lax.broadcasted_iota(jnp.int32, (32, 128), 0)
    ).astype(F32)
    for p in range(4):
        wide_b = jnp.dot(br[p].astype(F32), spread, preferred_element_type=F32)
        wide_f = jnp.dot(fl[p].astype(F32), spread, preferred_element_type=F32)
        cut = 1.0 - CRACK_CUT * jnp.where(low, wide_b[0:1, :], wide_b[1:2, :])
        on = jnp.where(low, wide_f[0:1, :], wide_f[1:2, :])
        for x in range(4 * p, 4 * p + 4):
            w = st[x] * cut
            wt[x] = w
            car[x] = 0.5 * on * w
            uu, rr, dd, to_up, to_dn = [], [], [], [], []
            for c in range(3):
                a = u[c, x]
                b = up[c, x]
                uu.append(a)
                rr.append((2.0 * a - b) + f[c, x])
                dd.append(a - b)
                rhs[c, x] = rr[c]
                dif[c, x] = dd[c]
            u1, w4, r1 = rot(uu[1], 4, 0), rot(w, 4, 0), rot(rr[1], 4, 0)
            to_up.append(jnp.where(low, u1, uu[0]))
            to_up.append(jnp.where(low, w4, uu[2]))
            to_up.append(jnp.where(low, r1, rr[0]))
            extra = jnp.where(sub == 0, rot(uu[0], -3, 0), jnp.where(sub == 1, rot(uu[1], -2, 0), jnp.where(sub == 2, rot(uu[2], -1, 0), w)))
            to_up.append(jnp.where(low, extra, rr[2]))
            to_up.append(jnp.where(sub >= 6, dd[0], jnp.where(sub >= 4, rot(dd[1], -2, 0), rot(dd[2], 4, 0))))
            to_dn.append(jnp.where(low, uu[0], u1))
            to_dn.append(jnp.where(low, uu[2], w4))
            to_dn.append(jnp.where(low, rr[0], r1))
            extra = jnp.where(sub == 4, uu[0], jnp.where(sub == 5, rot(uu[1], 1, 0), jnp.where(sub == 6, rot(uu[2], 2, 0), rot(w, 3, 0))))
            to_dn.append(jnp.where(low, rr[2], extra))
            to_dn.append(jnp.where(sub < 2, dd[0], jnp.where(sub < 4, rot(dd[1], 2, 0), rot(dd[2], 4, 0))))
            for t in range(5):
                near, at = pick(x, m_near, n_near)
                far, _ = pick(x, m_far, n_far)
                near[at, t] = jnp.where(even, to_up[t], to_dn[t])
                far[at, t] = jnp.where(even, to_dn[t], to_up[t])


def unpack(msgs, x, low, even):
    near, at = pick(x, msgs[0], msgs[2])
    far, _ = pick(x, msgs[1], msgs[3])
    h0, h1, h2, h3, h4 = (jnp.where(even, near[at, t], far[at, t]) for t in range(5))
    l0, l1, l2, l3, l4 = (jnp.where(even, far[at, t], near[at, t]) for t in range(5))
    u0 = jnp.where(low, h0, l0)
    u1 = rot(jnp.where(low, l0, h0), 4, 0)
    u2 = jnp.where(low, h1, l1)
    w = rot(jnp.where(low, l1, h1), 4, 0)
    r0 = jnp.where(low, h2, l2)
    r1 = rot(jnp.where(low, l2, h2), 4, 0)
    r2 = jnp.where(low, h3, l3)
    d0 = jnp.where(low, h4, l4)
    d1 = jnp.where(low, rot(h4, -2, 0), rot(l4, 2, 0))
    d2 = rot(jnp.where(low, l4, h4), 4, 0)
    return (u0, u1, u2), (r0, r1, r2), (d0, d1, d2), w


def face_slots():
    slots, at = {}, 0
    for name, comps, own, halo in (("u", 3, 5, 4), ("r", 3, 4, 3), ("d", 3, 2, 1), ("w", 1, 5, 4)):
        for c in range(comps):
            for k in range(own):
                slots[name, c, k, 0] = at
                at += 1
            for k in range(halo):
                slots[name, c, k, 1] = at
                at += 1
    return slots, at


SLOTS, N_SLOTS = face_slots()


def face_kernel(u, rhs, dif, wt, near, far, q_near, q_far):
    low = sub_iota() < 4
    even_y, even_x = is_even("grp"), is_even("slab")

    def tiles(k, x):
        out = {(name, c, k, 0): own[c, x] for name, own in (("u", u), ("r", rhs), ("d", dif)) for c in range(3)}
        out["w", 0, k, 0] = wt[x]
        if k < 4:
            hu, hr, hd, out["w", 0, k, 1] = unpack((near, far, None, None), x, low, even_y)
            for name, halo in (("u", hu), ("r", hr), ("d", hd)):
                out.update({(name, c, k, 1): halo[c] for c in range(3)})
        return out

    for k in range(5):
        to_up, to_dn = tiles(k, NB - 1 - k), tiles(k, k)
        for key in to_up:
            if key in SLOTS:
                q_near[SLOTS[key]] = jnp.where(even_x, to_up[key], to_dn[key])
                q_far[SLOTS[key]] = jnp.where(even_x, to_dn[key], to_up[key])


def roll_y_up(pair, sub):
    a, b = rot(pair[0], -1, 0), rot(pair[1], -1, 0)
    return jnp.where(sub == 7, b, a), jnp.where(sub == 7, a, b)


def roll_y_dn(pair, sub):
    a, b = rot(pair[0], 1, 0), rot(pair[1], 1, 0)
    return jnp.where(sub == 0, b, a), jnp.where(sub == 0, a, b)


def pair_of(ref, *lead):
    return ref[(*lead, slice(0, 8))], ref[(*lead, slice(8, 16))]


def put(ref, pair, *lead):
    ref[(*lead, slice(0, 8))] = pair[0]
    ref[(*lead, slice(8, 16))] = pair[1]


def krylov_kernel(u, rhs, dif, wt, near, far, near2, far2, q_near, q_far, ub, r0, r1, r2, r3, v0, v1, mom, ue, we, re, de, kk):
    even_y, even_x = is_even("grp"), is_even("slab")
    sub = sub_iota()
    lane = lax.broadcasted_iota(jnp.int32, (8, 128), 1)
    low = sub < 4
    zero = jnp.zeros((8, 128), F32)

    def faces(slot):
        a, b = q_near[slot], q_far[slot]
        return jnp.where(even_x, b, a), jnp.where(even_x, a, b)

    for k in range(5):
        for name, ref, h, lead in (("u", ue, 5, range(3)), ("r", re, 4, range(3)), ("d", de, 2, range(3)), ("w", we, 5, (None,))):
            for c in lead:
                at = c or 0
                if (name, at, k, 0) in SLOTS:
                    own = faces(SLOTS[name, at, k, 0])
                    halo = faces(SLOTS[name, at, k, 1]) if (name, at, k, 1) in SLOTS else (zero, zero)
                    where = () if c is None else (c,)
                    put(ref, (own[0], halo[0]), *where, h - 1 - k)
                    put(ref, (own[1], halo[1]), *where, h + NB + k)

    def fill(x):
        hu, hr, hd, hw = unpack((near, far, near2, far2), x, low, even_y)
        for c in range(3):
            put(ue, (u[c, x], hu[c]), c, x + 5)
            put(re, (rhs[c, x], hr[c]), c, x + 4)
            put(de, (dif[c, x], hd[c]), c, x + 2)
        put(we, (wt[x], hw), x + 5)

    for x in range(NB):
        fill(x)

    def edges(x, ends):
        w = pair_of(we, x + 5)
        wxp, wxm = pair_of(we, x + 6), pair_of(we, x + 4)
        wyp, wym = roll_y_up(w, sub), roll_y_dn(w, sub)
        if ends is not None:
            wyp = (wyp[0], jnp.where(sub == 3, ends[0], wyp[1]))
            wym = (wym[0], jnp.where(sub == 4, ends[1], wym[1]))
        for t in range(2):
            rows = slice(8 * t, 8 * t + 8)
            inside = jnp.where(w[t] > 0.0, 0.5 * SPRING_SHEAR, 0.0)
            wzp = jnp.where(lane == 127, 0.0, rot(w[t], -1, 1))
            wzm = jnp.where(lane == 0, 0.0, rot(w[t], 1, 1))
            xp, xm, yp, ym, zp, zm = ((w[t] + o) * inside for o in (wxp[t], wxm[t], wyp[t], wym[t], wzp, wzm))
            sums = (xp + xm, yp + ym, zp + zm)
            base = (1.0 - SHIFT) + (sums[0] + sums[1] + sums[2])
            for i, val in enumerate((xp, xm, yp, ym, jnp.where(lane == 127, 0.0, zp), jnp.where(lane == 0, 0.0, zm))):
                kk[i, x + 4, rows] = val
            for c in range(3):
                kk[6 + c, x + 4, rows] = base + 1.5 * sums[c]

    def extra_rows(x):
        (a, at), (b, _) = pick(x, near, near2), pick(x, far, far2)
        a, b = a[at, 3], b[at, 3]
        return jnp.where(even_y, a, b), jnp.where(even_y, b, a)

    def own_edges(x):
        h3, l3 = extra_rows(x)
        edges(x, (h3[7:8, :], l3[3:4, :]))

    def far_edges(i, carry):
        edges(i - 4, None)
        edges(i + NB, None)
        return carry

    lax.fori_loop(0, 4, far_edges, 0, unroll=True)
    for x in range(NB):
        own_edges(x)

    def apply_b(ref, h, x, tiles=(0, 1), ends=None):
        k = [[kk[i, x + 4, 8 * t : 8 * t + 8] if t in tiles else None for t in range(2)] for i in range(9)]
        out, mids = [], []
        for c in range(3):
            mid = pair_of(ref, c, x + h)
            yp, ym = roll_y_up(mid, sub), roll_y_dn(mid, sub)
            if ends is not None:
                yp = (yp[0], jnp.where(sub == 3, ends[0][c], yp[1]))
                ym = (ym[0], jnp.where(sub == 4, ends[1][c], ym[1]))
            res = [None, None]
            for t in tiles:
                rows = slice(8 * t, 8 * t + 8)
                sx = k[0][t] * ref[c, x + h + 1, rows] + k[1][t] * ref[c, x + h - 1, rows]
                sy = k[2][t] * yp[t] + k[3][t] * ym[t]
                sz = k[4][t] * rot(mid[t], -1, 1) + k[5][t] * rot(mid[t], 1, 1)
                res[t] = k[6 + c][t] * mid[t] - ((sx + sy) + (sz + 1.5 * (sx, sy, sz)[c]))
            out.append(res)
            mids.append(mid)
        return out, mids

    def first(x, ends, with_v):
        bu, mids = apply_b(ue, 5, x, ends=ends)
        for c in range(3):
            rh = pair_of(re, c, x + 4)
            res = [rh[t] - (bu[c][t] + SHIFT * mids[c][t]) for t in range(2)]
            put(r0, res, c, x + 4)
            if with_v:
                d = pair_of(de, c, x + 2)
                put(v0, [res[t] - d[t] for t in range(2)], c, x + 2)

    def first_own(x):
        h3, l3 = extra_rows(x)
        first(x, ([h3[4 + c : 5 + c, :] for c in range(3)], [l3[c : c + 1, :] for c in range(3)]), True)
        for c in range(3):
            put(ub, pair_of(ue, c, x + 5), c, x + 1)

    for x in (-4, -3, NB + 2, NB + 3):
        first(x, None, False)
    for x in (-2, -1, NB, NB + 1):
        first(x, None, True)
    for c in range(3):
        put(ub, pair_of(ue, c, 4), c, 0)
        put(ub, pair_of(ue, c, NB + 5), c, NB + 1)
    for x in range(NB):
        first_own(x)

    def power(src, h, dst):
        def row(x, carry):
            out, _ = apply_b(src, h, x)
            for c in range(3):
                put(dst, out[c], c, x + h - 1)
            return carry

        lax.fori_loop(1 - h, NB + h - 1, row, 0, unroll=True)

    power(r0, 4, r1)
    power(v0, 2, v1)
    power(r1, 3, r2)
    power(r2, 2, r3)

    def dots(x, acc):
        r4, _ = apply_b(r3, 1, x, tiles=(0,))
        v2, _ = apply_b(v1, 1, x, tiles=(0,))
        acc = list(acc)
        for c in range(3):
            a = [ref[c, x + h, 0:8] for ref, h in ((r0, 4), (r1, 3), (r2, 2), (r3, 1))] + [r4[c][0]]
            b = [v0[c, x + 2, 0:8], v1[c, x + 1, 0:8], v2[c][0]]
            terms = [a[k // 2] * a[(k + 1) // 2] for k in range(8)]
            terms += [b[(k + 1) // 2] * a[k // 2] for k in range(5)] + [b[2] * a[3]]
            terms += [b[k // 2] * b[(k + 1) // 2] for k in range(4)]
            acc = [s + t for s, t in zip(acc, terms)] if c or True else acc
        return tuple(acc)

    acc = lax.fori_loop(0, NB, dots, (zero,) * 18, unroll=True)
    lane_row = lax.broadcasted_iota(jnp.int32, (1, 128), 1)
    line = jnp.zeros((1, 128), F32)
    for k in range(18):
        line = jnp.where(lane_row == k, jnp.sum(jnp.sum(acc[k], axis=0, keepdims=True), axis=1, keepdims=True), line)
    mom[...] = jnp.broadcast_to(line, mom.shape)


def two_iterations(m):
    alpha = m[0] / (SHIFT * m[0] + m[1])
    p0, p1 = 1.0 - SHIFT * alpha, -alpha
    new = p0 * p0 * m[0] + 2.0 * p0 * p1 * m[1] + p1 * p1 * m[2]
    e0, e1 = p0 + new / m[0], p1
    d0 = e0 * e0 * m[0] + 2.0 * e0 * e1 * m[1] + e1 * e1 * m[2]
    d1 = e0 * e0 * m[1] + 2.0 * e0 * e1 * m[2] + e1 * e1 * m[3]
    again = new / (SHIFT * d0 + d1)
    return alpha + again * e0, again * e1


def product3(value, table):
    high, rest = split(value)
    dot = lambda a, b: jnp.dot(a, b, preferred_element_type=F32)
    return dot(high, table[0]) + (dot(rest, table[0]) + dot(high, table[1]))


def code_kernel(ub, r0, r1, r2, r3, v0, v1, mom, car, mix, tz, disp, code, uf, fl):
    sub = sub_iota()
    lane = lax.broadcasted_iota(jnp.int32, (8, 128), 1)
    total = jnp.sum(mom[...], axis=0, keepdims=True)
    lane_row = lax.broadcasted_iota(jnp.int32, (1, 128), 1)
    m = [jnp.sum(jnp.where(lane_row == k, total, 0.0), axis=1, keepdims=True) for k in range(18)]
    rr, vr, vv = m[:8], m[8:14], m[14:]
    a0, a1 = two_iterations(rr)
    g = (a0 * (2.0 - SHIFT), a1 * (2.0 - SHIFT) - a0, -a1)
    mix2 = []
    for k in range(4):
        s = vv[k]
        for i in range(3):
            s = s + 2.0 * g[i] * vr[k + i]
            for j in range(3):
                s = s + g[i] * g[j] * rr[k + i + j]
        mix2.append(s)
    b0, b1 = two_iterations(mix2)
    coef = [b0, b1, a0 + b0 * g[0], a1 + b0 * g[1] + b1 * g[0], b0 * g[2] + b1 * g[1], b1 * g[2]]
    coef = [jnp.broadcast_to(v, (8, 128)) for v in coef]
    parts = ((v0, 2), (v1, 1), (r0, 4), (r1, 3), (r2, 2), (r3, 1))

    def combine(i, carry):
        for c in range(3):
            for t in range(2):
                rows = slice(8 * t, 8 * t + 8)
                s = ub[c, i, rows]
                for w, (ref, h) in zip(coef, parts):
                    s = s + w * ref[c, i + h - 1, rows]
                uf[c, i, rows] = s
        return carry

    lax.fori_loop(0, NB + 2, combine, 0, unroll=True)

    def stress(x, carry):
        k = car[x]
        for c in range(3):
            own = uf[c, x + 1, 0:8]
            disp[c, x] = own
            fl[c, x] = own
        fl[3, x] = k * (uf[0, x + 2, 0:8] - uf[0, x, 0:8])
        y = pair_of(uf, 1, x + 1)
        fl[4, x] = k * (roll_y_up(y, sub)[0] - roll_y_dn(y, sub)[0])
        z = uf[2, x + 1, 0:8]
        fl[5, x] = k * (jnp.where(lane == 127, 0.0, rot(z, -1, 1)) - jnp.where(lane == 0, 0.0, rot(z, 1, 1)))
        return carry

    lax.fori_loop(0, NB, stress, 0, unroll=True)
    along_z = product3(fl[...].reshape(768, 128), tz)
    turned = jnp.concatenate([along_z[128 * ch : 128 * ch + 128].T for ch in range(6)], axis=0)
    done = product3(turned, mix)
    for ch in range(6):
        for i in range(16):
            code[pl.ds(48 * i + ch, 8, stride=6), :] = done[128 * ch + 8 * i : 128 * ch + 8 * i + 8]


def wavelet_kernel(got, w1, w2, w3, out, xs):
    sub = sub_iota()
    lane = lax.broadcasted_iota(jnp.int32, (8, 128), 1)
    for j in range(16):
        tiles = []
        for ch in range(6):
            tile = got[pl.ds(48 * j + ch, 8, stride=6), :]
            for b in range(3):
                step = 1 << b
                s_bit, l_bit = (sub // step) % 2, (lane // step) % 2
                up, down = rot(rot(tile, -step, 0), step, 1), rot(rot(tile, step, 0), -step, 1)
                tile = jnp.where(s_bit == l_bit, tile, jnp.where(s_bit == 0, up, down))
            tiles.append(tile)
        high, rest = split(jnp.concatenate(tiles, axis=0))
        xs[0, j] = high
        xs[1, j] = rest

    def product(first, step, count, weight):
        rows = [
            jnp.concatenate([xs[part, (first + step * q + t) % 16] for t in range(count)], axis=1)
            for part in range(2)
            for q in range(16 // step)
        ]
        both = jnp.dot(jnp.concatenate(rows, axis=0), weight[...], preferred_element_type=F32)
        half = both.shape[0] // 2
        return both[:half] + both[half:]

    def emit(value, tile):
        for ch in range(6):
            out[pl.ds(128 * ch + tile, 8, stride=16), :] = value[8 * ch : 8 * ch + 8]

    fine = product(0, 2, 3, w1)
    for q in range(8):
        emit(fine[48 * q : 48 * q + 48], 8 + q)
    middle = product(15, 4, 6, w2)
    for q in range(4):
        emit(middle[48 * q : 48 * q + 48], 4 + q)
    coarse = product(15, 8, 10, w3)
    for q in range(2):
        emit(coarse[48 * q : 48 * q + 48, :128], q)
        emit(coarse[48 * q : 48 * q + 48, 128:], 2 + q)


def call(kernel, outs, scratch=(), **specs):
    return pl.pallas_call(
        kernel,
        out_shape=[jax.ShapeDtypeStruct(s, F32) for s in outs],
        scratch_shapes=[pltpu.VMEM(s, F32) if isinstance(s, tuple) else s for s in scratch],
        **specs,
        compiler_params=pltpu.CompilerParams(vmem_limit_bytes=40 * 2**20),
    )


def swap(near, far, axis, count):
    both = lambda first: [p for i in range(first, count - 1, 2) for p in ((i, i + 1), (i + 1, i))]
    return lax.ppermute(near, axis, both(0)), lax.ppermute(far, axis, both(1))


def share(rows, axes, groups):
    count = len(groups[0])
    return lax.all_to_all(rows.reshape(count, 1, 128), axes, 0, 0, axis_index_groups=groups, tiled=True).reshape(count, 128)


def total_kernel(rows, out):
    out[...] = jnp.broadcast_to(jnp.sum(rows[...], axis=0, keepdims=True), out.shape)


def body(u_now, u_prev, force, stiffness, broken, flags):
    n_slab, n_grp = lax.axis_size("slab"), lax.axis_size("grp")
    planes = [[16 * y + k for k in range(16)] for y in range(n_slab // 16)]
    lines = [[(16 * y + k) * n_grp + g for y in range(n_slab // 16) for g in range(n_grp)] for k in range(16)]
    block, one = (3, NB, 8, 128), (NB, 8, 128)
    m_near, m_far, n_near, n_far, rhs, dif, wt, car, u_here = call(
        pack_kernel,
        [(NB // 2, 5, 8, 128)] * 2 + [(NB // 2, 9, 8, 128)] * 2 + [block, block, one, one, block],
        [block, block, one, pltpu.VMEM(broken.shape, jnp.int32), pltpu.VMEM(flags.shape, jnp.int32), pltpu.SemaphoreType.DMA((6,))],
        in_specs=[pl.BlockSpec(memory_space=pltpu.HBM)] * 6,
    )(*(pltpu.with_memory_space_constraint(v, pltpu.HBM) for v in (u_now, u_prev, force, stiffness, broken, flags)))
    m_near, m_far = swap(m_near, m_far, "grp", n_grp)
    n_near, n_far = swap(n_near, n_far, "grp", n_grp)
    q_near, q_far = call(face_kernel, [(N_SLOTS, 8, 128)] * 2)(u_here, rhs, dif, wt, m_near, m_far)
    q_near, q_far = swap(q_near, q_far, "slab", n_slab)
    wide = lambda h: (3, NB + 2 * h, 16, 128)
    *basis, mom = call(
        krylov_kernel,
        [wide(1), wide(4), wide(3), wide(2), wide(1), wide(2), wide(1), (len(lines[0]), 128)],
        [wide(5), wide(5)[1:], wide(4), wide(2), (9, NB + 8, 16, 128)],
    )(u_here, rhs, dif, wt, m_near, m_far, n_near, n_far, q_near, q_far)
    mom = share(mom, ("slab", "grp"), lines)
    (mom,) = call(total_kernel, [(len(planes[0]), 128)])(mom)
    mom = share(mom, "slab", planes)
    table = cosine_table()
    mix = two_parts(np.kron(np.kron(np.eye(4), table), np.kron(np.eye(2), table)).T)
    tz = two_parts(np.kron(np.eye(32), table).T)
    disp, code = call(
        code_kernel, [block, (768, 128)], [wide(1), (6, NB, 8, 128)]
    )(*basis, mom, car, mix, tz)
    got = lax.all_to_all(code.reshape(n_slab, 1, 768), "slab", 0, 0, tiled=True).reshape(768, 128)
    (coeffs,) = call(wavelet_kernel, [(768, 128)], [pltpu.VMEM((2, 16, 48, 128), BF16)])(got, *(jnp.asarray(w, BF16) for w in wavelet_tables()))
    return (disp, coeffs.reshape(6, 8, 1, 2048))


def solution(mesh):
    return jax.shard_map(
        body,
        mesh=mesh,
        in_specs=(
            P(None, "slab", "grp", None),
            P(None, "slab", "grp", None),
            P(None, "slab", "grp", None),
            P("slab", "grp", None),
            P("slab", "grp", None),
            P("slab", "grp", None),
        ),
        out_specs=(P(None, "slab", "grp", None), P(None, "grp", "slab", None)),
        check_vma=False,
    )
```

```python
import jax
import jax.numpy as jnp
import numpy as np
from jax import lax
from jax.experimental import pallas as pl
from jax.experimental.pallas import tpu as pltpu
from jax.sharding import PartitionSpec as P

SPRING_SHEAR = 0.4
CRACK_CUT = 0.9
SHIFT = 2.5
F32 = jnp.float32
BF16 = jnp.bfloat16
NB = 16


def cosine_table():
    freq = np.arange(4)[:, None]
    place = np.arange(4)[None, :]
    factor = np.where(freq == 0, 0.5, np.sqrt(0.5))
    return factor * np.cos(np.pi * (2 * place + 1) * freq / 8.0)


def lift_np(signal):
    even, odd = signal[..., 0::2], signal[..., 1::2]
    detail = odd - 0.5 * (even + np.roll(even, -1, axis=-1))
    approx = even + 0.25 * (np.roll(detail, 1, axis=-1) + detail)
    return approx, detail


def wavelet_tables():
    size = 2048
    eye = np.eye(size)
    a1, d1 = lift_np(eye)
    a2, d2 = lift_np(a1)
    a3, d3 = lift_np(a2)
    lane = np.arange(128)
    place = (lane % 8) * 16 + lane // 8

    def rows(first, count):
        return np.concatenate([((first + t) % 16) * 128 + place for t in range(count)])

    w1 = d1[rows(0, 3)][:, :128]
    w2 = d2[rows(3, 6)][:, 128:256]
    w3 = np.concatenate([a3[rows(7, 10)][:, 128:], d3[rows(7, 10)][:, 128:]], axis=1)
    return [np.asarray(w, np.float32) for w in (w1, w2, w3)]


def two_parts(table):
    high = np.asarray(table, BF16)
    return jnp.stack([jnp.asarray(high), jnp.asarray(np.asarray(table - high.astype(np.float64), BF16))])


def sub_iota():
    return lax.broadcasted_iota(jnp.int32, (8, 128), 0)


def split(value):
    high = value.astype(BF16)
    return high, (value - high.astype(F32)).astype(BF16)


def rot(tile, shift, axis):
    return pltpu.roll(tile, shift % tile.shape[axis], axis)


def pick(x, outer, inner):
    if 4 <= x < NB - 4:
        return inner, x - 4
    return outer, x if x < 4 else x - 8


def is_even(axis):
    return lax.axis_index(axis) % 2 == 0


def pack_kernel(u_in, up_in, f_in, st_in, br_in, fl_in, m_near, m_far, n_near, n_far, rhs, dif, wt, car, u, up, f, st, br, fl, sems):
    pairs = ((br_in, br), (fl_in, fl), (st_in, st), (u_in, u), (up_in, up), (f_in, f))
    copies = [pltpu.make_async_copy(a, b, sems.at[i]) for i, (a, b) in enumerate(pairs)]
    for copy in copies:
        copy.start()
    for copy in copies:
        copy.wait()
    sub = sub_iota()
    low = sub < 4
    even = is_even("grp")
    n_near[:, 5:] = jnp.zeros((NB // 2, 4, 8, 128), F32)
    n_far[:, 5:] = jnp.zeros((NB // 2, 4, 8, 128), F32)
    spread = (
        lax.broadcasted_iota(jnp.int32, (32, 128), 1) // 4
        == lax.broadcasted_iota(jnp.int32, (32, 128), 0)
    ).astype(F32)
    for p in range(4):
        wide_b = jnp.dot(br[p].astype(F32), spread, preferred_element_type=F32)
        wide_f = jnp.dot(fl[p].astype(F32), spread, preferred_element_type=F32)
        cut = 1.0 - CRACK_CUT * jnp.where(low, wide_b[0:1, :], wide_b[1:2, :])
        on = jnp.where(low, wide_f[0:1, :], wide_f[1:2, :])
        for x in range(4 * p, 4 * p + 4):
            w = st[x] * cut
            wt[x] = w
            car[x] = 0.5 * on * w
            uu, rr, dd, to_up, to_dn = [], [], [], [], []
            for c in range(3):
                a = u[c, x]
                b = up[c, x]
                uu.append(a)
                rr.append((2.0 * a - b) + f[c, x])
                dd.append(a - b)
                rhs[c, x] = rr[c]
                dif[c, x] = dd[c]
            u1, w4, r1 = rot(uu[1], 4, 0), rot(w, 4, 0), rot(rr[1], 4, 0)
            to_up.append(jnp.where(low, u1, uu[0]))
            to_up.append(jnp.where(low, w4, uu[2]))
            to_up.append(jnp.where(low, r1, rr[0]))
            extra = jnp.where(sub == 0, rot(uu[0], -3, 0), jnp.where(sub == 1, rot(uu[1], -2, 0), jnp.where(sub == 2, rot(uu[2], -1, 0), w)))
            to_up.append(jnp.where(low, extra, rr[2]))
            to_up.append(jnp.where(sub >= 6, dd[0], jnp.where(sub >= 4, rot(dd[1], -2, 0), rot(dd[2], 4, 0))))
            to_dn.append(jnp.where(low, uu[0], u1))
            to_dn.append(jnp.where(low, uu[2], w4))
            to_dn.append(jnp.where(low, rr[0], r1))
            extra = jnp.where(sub == 4, uu[0], jnp.where(sub == 5, rot(uu[1], 1, 0), jnp.where(sub == 6, rot(uu[2], 2, 0), rot(w, 3, 0))))
            to_dn.append(jnp.where(low, rr[2], extra))
            to_dn.append(jnp.where(sub < 2, dd[0], jnp.where(sub < 4, rot(dd[1], 2, 0), rot(dd[2], 4, 0))))
            for t in range(5):
                near, at = pick(x, m_near, n_near)
                far, _ = pick(x, m_far, n_far)
                near[at, t] = jnp.where(even, to_up[t], to_dn[t])
                far[at, t] = jnp.where(even, to_dn[t], to_up[t])


def unpack(msgs, x, low, even):
    near, at = pick(x, msgs[0], msgs[2])
    far, _ = pick(x, msgs[1], msgs[3])
    h0, h1, h2, h3, h4 = (jnp.where(even, near[at, t], far[at, t]) for t in range(5))
    l0, l1, l2, l3, l4 = (jnp.where(even, far[at, t], near[at, t]) for t in range(5))
    u0 = jnp.where(low, h0, l0)
    u1 = rot(jnp.where(low, l0, h0), 4, 0)
    u2 = jnp.where(low, h1, l1)
    w = rot(jnp.where(low, l1, h1), 4, 0)
    r0 = jnp.where(low, h2, l2)
    r1 = rot(jnp.where(low, l2, h2), 4, 0)
    r2 = jnp.where(low, h3, l3)
    d0 = jnp.where(low, h4, l4)
    d1 = jnp.where(low, rot(h4, -2, 0), rot(l4, 2, 0))
    d2 = rot(jnp.where(low, l4, h4), 4, 0)
    return (u0, u1, u2), (r0, r1, r2), (d0, d1, d2), w


def face_slots():
    slots, at = {}, 0
    for name, comps, own, halo in (("u", 3, 5, 4), ("r", 3, 4, 3), ("d", 3, 2, 1), ("w", 1, 5, 4)):
        for c in range(comps):
            for k in range(own):
                slots[name, c, k, 0] = at
                at += 1
            for k in range(halo):
                slots[name, c, k, 1] = at
                at += 1
    return slots, at


SLOTS, N_SLOTS = face_slots()


def face_kernel(u, rhs, dif, wt, near, far, q_near, q_far):
    low = sub_iota() < 4
    even_y, even_x = is_even("grp"), is_even("slab")

    def tiles(k, x):
        out = {(name, c, k, 0): own[c, x] for name, own in (("u", u), ("r", rhs), ("d", dif)) for c in range(3)}
        out["w", 0, k, 0] = wt[x]
        if k < 4:
            hu, hr, hd, out["w", 0, k, 1] = unpack((near, far, None, None), x, low, even_y)
            for name, halo in (("u", hu), ("r", hr), ("d", hd)):
                out.update({(name, c, k, 1): halo[c] for c in range(3)})
        return out

    for k in range(5):
        to_up, to_dn = tiles(k, NB - 1 - k), tiles(k, k)
        for key in to_up:
            if key in SLOTS:
                q_near[SLOTS[key]] = jnp.where(even_x, to_up[key], to_dn[key])
                q_far[SLOTS[key]] = jnp.where(even_x, to_dn[key], to_up[key])


def roll_y_up(pair, sub):
    a, b = rot(pair[0], -1, 0), rot(pair[1], -1, 0)
    return jnp.where(sub == 7, b, a), jnp.where(sub == 7, a, b)


def roll_y_dn(pair, sub):
    a, b = rot(pair[0], 1, 0), rot(pair[1], 1, 0)
    return jnp.where(sub == 0, b, a), jnp.where(sub == 0, a, b)


def pair_of(ref, *lead):
    return ref[(*lead, slice(0, 8))], ref[(*lead, slice(8, 16))]


def put(ref, pair, *lead):
    ref[(*lead, slice(0, 8))] = pair[0]
    ref[(*lead, slice(8, 16))] = pair[1]


def krylov_kernel(u, rhs, dif, wt, near, far, near2, far2, q_near, q_far, ub, r0, r1, r2, r3, v0, v1, mom, ue, we, re, de, kk):
    even_y, even_x = is_even("grp"), is_even("slab")
    sub = sub_iota()
    lane = lax.broadcasted_iota(jnp.int32, (8, 128), 1)
    low = sub < 4
    zero = jnp.zeros((8, 128), F32)

    def faces(slot):
        a, b = q_near[slot], q_far[slot]
        return jnp.where(even_x, b, a), jnp.where(even_x, a, b)

    for k in range(5):
        for name, ref, h, lead in (("u", ue, 5, range(3)), ("r", re, 4, range(3)), ("d", de, 2, range(3)), ("w", we, 5, (None,))):
            for c in lead:
                at = c or 0
                if (name, at, k, 0) in SLOTS:
                    own = faces(SLOTS[name, at, k, 0])
                    halo = faces(SLOTS[name, at, k, 1]) if (name, at, k, 1) in SLOTS else (zero, zero)
                    where = () if c is None else (c,)
                    put(ref, (own[0], halo[0]), *where, h - 1 - k)
                    put(ref, (own[1], halo[1]), *where, h + NB + k)

    def fill(x):
        hu, hr, hd, hw = unpack((near, far, near2, far2), x, low, even_y)
        for c in range(3):
            put(ue, (u[c, x], hu[c]), c, x + 5)
            put(re, (rhs[c, x], hr[c]), c, x + 4)
            put(de, (dif[c, x], hd[c]), c, x + 2)
        put(we, (wt[x], hw), x + 5)

    for x in range(NB):
        fill(x)

    def edges(x, ends):
        w = pair_of(we, x + 5)
        wxp, wxm = pair_of(we, x + 6), pair_of(we, x + 4)
        wyp, wym = roll_y_up(w, sub), roll_y_dn(w, sub)
        if ends is not None:
            wyp = (wyp[0], jnp.where(sub == 3, ends[0], wyp[1]))
            wym = (wym[0], jnp.where(sub == 4, ends[1], wym[1]))
        for t in range(2):
            rows = slice(8 * t, 8 * t + 8)
            inside = jnp.where(w[t] > 0.0, 0.5 * SPRING_SHEAR, 0.0)
            wzp = jnp.where(lane == 127, 0.0, rot(w[t], -1, 1))
            wzm = jnp.where(lane == 0, 0.0, rot(w[t], 1, 1))
            xp, xm, yp, ym, zp, zm = ((w[t] + o) * inside for o in (wxp[t], wxm[t], wyp[t], wym[t], wzp, wzm))
            sums = (xp + xm, yp + ym, zp + zm)
            base = (1.0 - SHIFT) + (sums[0] + sums[1] + sums[2])
            for i, val in enumerate((xp, xm, yp, ym, jnp.where(lane == 127, 0.0, zp), jnp.where(lane == 0, 0.0, zm))):
                kk[i, x + 4, rows] = val
            for c in range(3):
                kk[6 + c, x + 4, rows] = base + 1.5 * sums[c]

    def extra_rows(x):
        (a, at), (b, _) = pick(x, near, near2), pick(x, far, far2)
        a, b = a[at, 3], b[at, 3]
        return jnp.where(even_y, a, b), jnp.where(even_y, b, a)

    def own_edges(x):
        h3, l3 = extra_rows(x)
        edges(x, (h3[7:8, :], l3[3:4, :]))

    def far_edges(i, carry):
        edges(i - 4, None)
        edges(i + NB, None)
        return carry

    lax.fori_loop(0, 4, far_edges, 0, unroll=True)
    for x in range(NB):
        own_edges(x)

    def apply_b(ref, h, x, tiles=(0, 1), ends=None):
        k = [[kk[i, x + 4, 8 * t : 8 * t + 8] if t in tiles else None for t in range(2)] for i in range(9)]
        out, mids = [], []
        for c in range(3):
            mid = pair_of(ref, c, x + h)
            yp, ym = roll_y_up(mid, sub), roll_y_dn(mid, sub)
            if ends is not None:
                yp = (yp[0], jnp.where(sub == 3, ends[0][c], yp[1]))
                ym = (ym[0], jnp.where(sub == 4, ends[1][c], ym[1]))
            res = [None, None]
            for t in tiles:
                rows = slice(8 * t, 8 * t + 8)
                sx = k[0][t] * ref[c, x + h + 1, rows] + k[1][t] * ref[c, x + h - 1, rows]
                sy = k[2][t] * yp[t] + k[3][t] * ym[t]
                sz = k[4][t] * rot(mid[t], -1, 1) + k[5][t] * rot(mid[t], 1, 1)
                res[t] = k[6 + c][t] * mid[t] - ((sx + sy) + (sz + 1.5 * (sx, sy, sz)[c]))
            out.append(res)
            mids.append(mid)
        return out, mids

    def first(x, ends, with_v):
        bu, mids = apply_b(ue, 5, x, ends=ends)
        for c in range(3):
            rh = pair_of(re, c, x + 4)
            res = [rh[t] - (bu[c][t] + SHIFT * mids[c][t]) for t in range(2)]
            put(r0, res, c, x + 4)
            if with_v:
                d = pair_of(de, c, x + 2)
                put(v0, [res[t] - d[t] for t in range(2)], c, x + 2)

    def first_own(x):
        h3, l3 = extra_rows(x)
        first(x, ([h3[4 + c : 5 + c, :] for c in range(3)], [l3[c : c + 1, :] for c in range(3)]), True)
        for c in range(3):
            put(ub, pair_of(ue, c, x + 5), c, x + 1)

    for x in (-4, -3, NB + 2, NB + 3):
        first(x, None, False)
    for x in (-2, -1, NB, NB + 1):
        first(x, None, True)
    for c in range(3):
        put(ub, pair_of(ue, c, 4), c, 0)
        put(ub, pair_of(ue, c, NB + 5), c, NB + 1)
    for x in range(NB):
        first_own(x)

    def power(src, h, dst):
        def row(x, carry):
            out, _ = apply_b(src, h, x)
            for c in range(3):
                put(dst, out[c], c, x + h - 1)
            return carry

        lax.fori_loop(1 - h, NB + h - 1, row, 0, unroll=True)

    power(r0, 4, r1)
    power(v0, 2, v1)
    power(r1, 3, r2)
    power(r2, 2, r3)

    def dots(x, acc):
        r4, _ = apply_b(r3, 1, x, tiles=(0,))
        v2, _ = apply_b(v1, 1, x, tiles=(0,))
        acc = list(acc)
        for c in range(3):
            a = [ref[c, x + h, 0:8] for ref, h in ((r0, 4), (r1, 3), (r2, 2), (r3, 1))] + [r4[c][0]]
            b = [v0[c, x + 2, 0:8], v1[c, x + 1, 0:8], v2[c][0]]
            terms = [a[k // 2] * a[(k + 1) // 2] for k in range(8)]
            terms += [b[(k + 1) // 2] * a[k // 2] for k in range(5)] + [b[2] * a[3]]
            terms += [b[k // 2] * b[(k + 1) // 2] for k in range(4)]
            acc = [s + t for s, t in zip(acc, terms)] if c or True else acc
        return tuple(acc)

    acc = lax.fori_loop(0, NB, dots, (zero,) * 18, unroll=True)
    lane_row = lax.broadcasted_iota(jnp.int32, (1, 128), 1)
    line = jnp.zeros((1, 128), F32)
    for k in range(18):
        line = jnp.where(lane_row == k, jnp.sum(jnp.sum(acc[k], axis=0, keepdims=True), axis=1, keepdims=True), line)
    mom[...] = jnp.broadcast_to(line, mom.shape)


def two_iterations(m):
    alpha = m[0] / (SHIFT * m[0] + m[1])
    p0, p1 = 1.0 - SHIFT * alpha, -alpha
    new = p0 * p0 * m[0] + 2.0 * p0 * p1 * m[1] + p1 * p1 * m[2]
    e0, e1 = p0 + new / m[0], p1
    d0 = e0 * e0 * m[0] + 2.0 * e0 * e1 * m[1] + e1 * e1 * m[2]
    d1 = e0 * e0 * m[1] + 2.0 * e0 * e1 * m[2] + e1 * e1 * m[3]
    again = new / (SHIFT * d0 + d1)
    return alpha + again * e0, again * e1


def product3(value, table):
    high, rest = split(value)
    dot = lambda a, b: jnp.dot(a, b, preferred_element_type=F32)
    return dot(high, table[0]) + (dot(rest, table[0]) + dot(high, table[1]))


def code_kernel(ub, r0, r1, r2, r3, v0, v1, mom, car, mix, tz, disp, code, uf, fl, sem):
    sub = sub_iota()
    lane = lax.broadcasted_iota(jnp.int32, (8, 128), 1)
    total = jnp.sum(mom[...], axis=0, keepdims=True)
    lane_row = lax.broadcasted_iota(jnp.int32, (1, 128), 1)
    m = [jnp.sum(jnp.where(lane_row == k, total, 0.0), axis=1, keepdims=True) for k in range(18)]
    rr, vr, vv = m[:8], m[8:14], m[14:]
    a0, a1 = two_iterations(rr)
    g = (a0 * (2.0 - SHIFT), a1 * (2.0 - SHIFT) - a0, -a1)
    mix2 = []
    for k in range(4):
        s = vv[k]
        for i in range(3):
            s = s + 2.0 * g[i] * vr[k + i]
            for j in range(3):
                s = s + g[i] * g[j] * rr[k + i + j]
        mix2.append(s)
    b0, b1 = two_iterations(mix2)
    coef = [b0, b1, a0 + b0 * g[0], a1 + b0 * g[1] + b1 * g[0], b0 * g[2] + b1 * g[1], b1 * g[2]]
    coef = [jnp.broadcast_to(v, (8, 128)) for v in coef]
    parts = ((v0, 2), (v1, 1), (r0, 4), (r1, 3), (r2, 2), (r3, 1))

    def combine(i, carry):
        for c in range(3):
            for t in range(2):
                rows = slice(8 * t, 8 * t + 8)
                s = ub[c, i, rows]
                for w, (ref, h) in zip(coef, parts):
                    s = s + w * ref[c, i + h - 1, rows]
                uf[c, i, rows] = s
        return carry

    lax.fori_loop(0, NB + 2, combine, 0, unroll=True)

    def stress(x, carry):
        k = car[x]
        for c in range(3):
            own = uf[c, x + 1, 0:8]
            fl[c, x] = own
        fl[3, x] = k * (uf[0, x + 2, 0:8] - uf[0, x, 0:8])
        y = pair_of(uf, 1, x + 1)
        fl[4, x] = k * (roll_y_up(y, sub)[0] - roll_y_dn(y, sub)[0])
        z = uf[2, x + 1, 0:8]
        fl[5, x] = k * (jnp.where(lane == 127, 0.0, rot(z, -1, 1)) - jnp.where(lane == 0, 0.0, rot(z, 1, 1)))
        return carry

    lax.fori_loop(0, NB, stress, 0, unroll=True)
    sent = pltpu.make_async_copy(fl.at[0:3], disp, sem)
    sent.start()
    along_z = product3(fl[...].reshape(768, 128), tz)
    turned = jnp.concatenate([along_z[128 * ch : 128 * ch + 128].T for ch in range(6)], axis=0)
    done = product3(turned, mix)
    for ch in range(6):
        for i in range(16):
            code[pl.ds(48 * i + ch, 8, stride=6), :] = done[128 * ch + 8 * i : 128 * ch + 8 * i + 8]
    sent.wait()


def wavelet_kernel(got, w1, w2, w3, out, xs):
    sub = sub_iota()
    lane = lax.broadcasted_iota(jnp.int32, (8, 128), 1)
    for j in range(16):
        tiles = []
        for ch in range(6):
            tile = got[pl.ds(48 * j + ch, 8, stride=6), :]
            for b in range(3):
                step = 1 << b
                s_bit, l_bit = (sub // step) % 2, (lane // step) % 2
                up, down = rot(rot(tile, -step, 0), step, 1), rot(rot(tile, step, 0), -step, 1)
                tile = jnp.where(s_bit == l_bit, tile, jnp.where(s_bit == 0, up, down))
            tiles.append(tile)
        high, rest = split(jnp.concatenate(tiles, axis=0))
        xs[0, j] = high
        xs[1, j] = rest

    def product(first, step, count, weight):
        rows = [
            jnp.concatenate([xs[part, (first + step * q + t) % 16] for t in range(count)], axis=1)
            for part in range(2)
            for q in range(16 // step)
        ]
        both = jnp.dot(jnp.concatenate(rows, axis=0), weight[...], preferred_element_type=F32)
        half = both.shape[0] // 2
        return both[:half] + both[half:]

    def emit(value, tile):
        for ch in range(6):
            out[pl.ds(128 * ch + tile, 8, stride=16), :] = value[8 * ch : 8 * ch + 8]

    fine = product(0, 2, 3, w1)
    for q in range(8):
        emit(fine[48 * q : 48 * q + 48], 8 + q)
    middle = product(15, 4, 6, w2)
    for q in range(4):
        emit(middle[48 * q : 48 * q + 48], 4 + q)
    coarse = product(15, 8, 10, w3)
    for q in range(2):
        emit(coarse[48 * q : 48 * q + 48, :128], q)
        emit(coarse[48 * q : 48 * q + 48, 128:], 2 + q)


def call(kernel, outs, scratch=(), **specs):
    return pl.pallas_call(
        kernel,
        out_shape=[jax.ShapeDtypeStruct(s, F32) for s in outs],
        scratch_shapes=[pltpu.VMEM(s, F32) if isinstance(s, tuple) else s for s in scratch],
        **specs,
        compiler_params=pltpu.CompilerParams(vmem_limit_bytes=40 * 2**20),
    )


def swap(near, far, axis, count):
    both = lambda first: [p for i in range(first, count - 1, 2) for p in ((i, i + 1), (i + 1, i))]
    return lax.ppermute(near, axis, both(0)), lax.ppermute(far, axis, both(1))


def share(rows, axes, groups):
    count = len(groups[0])
    return lax.all_to_all(rows.reshape(count, 1, 128), axes, 0, 0, axis_index_groups=groups, tiled=True).reshape(count, 128)


def total_kernel(rows, out):
    out[...] = jnp.broadcast_to(jnp.sum(rows[...], axis=0, keepdims=True), out.shape)


def body(u_now, u_prev, force, stiffness, broken, flags):
    n_slab, n_grp = lax.axis_size("slab"), lax.axis_size("grp")
    planes = [[16 * y + k for k in range(16)] for y in range(n_slab // 16)]
    lines = [[(16 * y + k) * n_grp + g for y in range(n_slab // 16) for g in range(n_grp)] for k in range(16)]
    block, one = (3, NB, 8, 128), (NB, 8, 128)
    m_near, m_far, n_near, n_far, rhs, dif, wt, car, u_here = call(
        pack_kernel,
        [(NB // 2, 5, 8, 128)] * 2 + [(NB // 2, 9, 8, 128)] * 2 + [block, block, one, one, block],
        [block, block, one, pltpu.VMEM(broken.shape, jnp.int32), pltpu.VMEM(flags.shape, jnp.int32), pltpu.SemaphoreType.DMA((6,))],
        in_specs=[pl.BlockSpec(memory_space=pltpu.HBM)] * 6,
    )(*(pltpu.with_memory_space_constraint(v, pltpu.HBM) for v in (u_now, u_prev, force, stiffness, broken, flags)))
    m_near, m_far = swap(m_near, m_far, "grp", n_grp)
    n_near, n_far = swap(n_near, n_far, "grp", n_grp)
    q_near, q_far = call(face_kernel, [(N_SLOTS, 8, 128)] * 2)(u_here, rhs, dif, wt, m_near, m_far)
    q_near, q_far = swap(q_near, q_far, "slab", n_slab)
    wide = lambda h: (3, NB + 2 * h, 16, 128)
    *basis, mom = call(
        krylov_kernel,
        [wide(1), wide(4), wide(3), wide(2), wide(1), wide(2), wide(1), (len(lines[0]), 128)],
        [wide(5), wide(5)[1:], wide(4), wide(2), (9, NB + 8, 16, 128)],
    )(u_here, rhs, dif, wt, m_near, m_far, n_near, n_far, q_near, q_far)
    mom = share(mom, ("slab", "grp"), lines)
    (mom,) = call(total_kernel, [(len(planes[0]), 128)])(mom)
    mom = share(mom, "slab", planes)
    table = cosine_table()
    mix = two_parts(np.kron(np.kron(np.eye(4), table), np.kron(np.eye(2), table)).T)
    tz = two_parts(np.kron(np.eye(32), table).T)
    disp, code = call(
        code_kernel, [block, (768, 128)], [wide(1), (6, NB, 8, 128), pltpu.SemaphoreType.DMA], out_specs=[pl.BlockSpec(memory_space=pltpu.HBM), pl.BlockSpec(memory_space=pltpu.VMEM)],
    )(*basis, mom, car, mix, tz)
    got = lax.all_to_all(code.reshape(n_slab, 1, 768), "slab", 0, 0, tiled=True).reshape(768, 128)
    (coeffs,) = call(wavelet_kernel, [(768, 128)], [pltpu.VMEM((2, 16, 48, 128), BF16)])(got, *(jnp.asarray(w, BF16) for w in wavelet_tables()))
    return (disp, coeffs.reshape(6, 8, 1, 2048))


def solution(mesh):
    return jax.shard_map(
        body,
        mesh=mesh,
        in_specs=(
            P(None, "slab", "grp", None),
            P(None, "slab", "grp", None),
            P(None, "slab", "grp", None),
            P("slab", "grp", None),
            P("slab", "grp", None),
            P("slab", "grp", None),
        ),
        out_specs=(P(None, "slab", "grp", None), P(None, "grp", "slab", None)),
        check_vma=False,
    )
```
